256 devices in a mesh: aux: 32 (over y, x, core), orb: 8 (over z).
Axes of the slice: x: 4, y: 4, z: 8, core: 2. Of those that a mesh axis runs over, the one named last changes fastest.
Arguments:
- tiles: float32 [2048, 64, 4096], P(('aux', 'orb')), may hold values from -6 to 6
- tile_list: int32 [4, 2048], P(None, ('aux', 'orb')), may hold values from 0 to 255, as said below
- orb_factor: float32 [4096, 256], P('orb'), may hold values from -30 to 30
- nu_factor: float32 [512, 256], replicated, may hold values from -30 to 30
Outputs:
- aux_factor: float32 [16384, 256], P('aux')
- orb_updated: float32 [4096, 256], P('orb')
- nu_updated: float32 [512, 256], replicated
The draws below stay inside these ranges and needn't reach their ends.
Inputs may be any that keep to these rules, and one draw needn't show every extreme that they name: `tile_list`: slot s belongs to the device s // 8 along aux+orb; for that device with aux index a and orb index o, row 0 lies in [a * 8, (a + 1) * 8), row 1 in [o * 8, (o + 1) * 8), row 2 below 8. The coordinates of one device's slots are distinct. Row 3 is 0 or 1: 1 on a device's first slots and 0 on the rest; every device has at least one flagged slot and some device has all 8 flagged.
All inputs are finite; a program needn't handle non-finite values.
Results may differ from the reference program's by a relative error of at most 0.0003.
Values sent between devices are 32-bit elements; how exact they have to be, the bound alone decides.
No kernel may reach another device: no remote copies, remote signals or barrier semaphores. Data moves between devices by JAX's collectives and lax.ppermute only.
A program may use at most 256 MiB of HBM per device.

```python
import jax
import jax.numpy as jnp
from jax import lax

P_SIZE = 16384
MU = 4096
NU = 512
R = 256
TILE = 64
TILES_DEV = 8
NTILES = 2048
BLOCK_P = 8
BLOCK_M = 8


def factor_draw(key, row_count):
    key_list = jax.random.split(key, 4)
    noise_part = jnp.clip(jax.random.normal(key_list[0], (row_count, R), jnp.float32), -4.0, 4.0)
    shared = jnp.clip(jax.random.normal(key_list[1], (row_count, 12), jnp.float32), -4.0, 4.0)
    amplitudes = jax.random.uniform(key_list[2], (12, 1), jnp.float32, 0.3, 1.5)
    mixing = jax.random.normal(key_list[3], (12, R), jnp.float32) * amplitudes
    values = noise_part + jnp.dot(shared, mixing, preferred_element_type=jnp.float32)
    return jnp.clip(values, -30.0, 30.0)


def draw_orb_factor(key, part):
    return factor_draw(jax.random.fold_in(key, 11), MU)


def draw_nu_factor(key, part):
    return factor_draw(jax.random.fold_in(key, 13), NU)


def draw_tile_list(key, part):
    devices_all = NTILES // TILES_DEV
    orb_span = MU // TILE // BLOCK_M
    nu_tiles = NU // TILE
    region = BLOCK_P * BLOCK_M * nu_tiles
    key_list = jax.random.split(jax.random.fold_in(key, 7), 4)

    def pick_cells(device_key):
        return jax.random.permutation(device_key, region)[:TILES_DEV]
    cell_ids = jax.vmap(pick_cells)(jax.random.split(key_list[0], devices_all)).astype(jnp.int32)
    device_ids = jnp.arange(devices_all, dtype=jnp.int32)[:, None]
    shifted = (cell_ids + (region - 1 - cell_ids[:, :1])) % region
    is_last = device_ids == devices_all - 1
    cell_ids = jnp.where(is_last, shifted, cell_ids).astype(jnp.int32)
    first_tile = device_ids // orb_span * BLOCK_P + cell_ids // (BLOCK_M * nu_tiles)
    second_tile = device_ids % orb_span * BLOCK_M + cell_ids // nu_tiles % BLOCK_M
    third_tile = cell_ids % nu_tiles
    top_count = max(1, TILES_DEV // 2)
    counts = jax.random.randint(key_list[1], (devices_all, 1), 1, top_count + 1)
    picked_full = jax.random.randint(key_list[2], (devices_all, 1), 0, 8) == 0
    chosen = jax.random.randint(key_list[3], (), 0, devices_all)
    filled = picked_full | (device_ids == chosen)
    counts = jnp.where(filled, TILES_DEV, counts)
    slot_ids = jnp.arange(TILES_DEV, dtype=jnp.int32)[None, :]
    live_flags = (slot_ids < counts).astype(jnp.int32)
    stacked = jnp.stack([first_tile, second_tile, third_tile, live_flags])
    return stacked.reshape(4, NTILES).astype(jnp.int32)


def levels(stream_key, dims, pieces, least, top_value):
    gain, own = 1.0, jax.random.fold_in(stream_key, 6)
    for position, parts in pieces:
        draws = jnp.exp(jax.random.uniform(jax.random.fold_in(own, position), (parts,), jnp.float32, least / len(pieces), top_value / len(pieces)))
        gain = gain * jnp.repeat(draws, dims[position] // parts).reshape([-1 if axis == position else 1 for axis in range(len(dims))])
    return gain


def gaussian(key, dims, spread, limit, cuts=(), kind=jnp.bfloat16):
    factor_of = levels(key, dims, cuts, -0.22, 0.18) if cuts else 1.0
    result = jax.random.normal(key, dims, jnp.float32) * spread * factor_of
    return jnp.minimum(jnp.maximum(result, -limit), limit).astype(kind)


def setup_inputs(seed: int = 0) -> dict:
    key_of = jax.random.split(jax.random.key(seed), 5)
    tiles = gaussian(key_of[0], (NTILES, TILE, TILE * TILE), 1.0, 6.0, ((0, 256),), jnp.float32)
    tile_list = draw_tile_list(jax.random.fold_in(key_of[4], 71), 0)
    orb_factor = draw_orb_factor(jax.random.fold_in(key_of[4], 71), 0)
    nu_factor = draw_nu_factor(jax.random.fold_in(key_of[4], 71), 0)
    return {"tiles": tiles, "tile_list": tile_list, "orb_factor": orb_factor, "nu_factor": nu_factor}


ridge_weight = 0.5
epsilon = 1e-06
highest = lax.Precision.HIGHEST

def gram_of(matrix):
    return jnp.dot(matrix.T.astype(jnp.float32), matrix.astype(jnp.float32), precision=highest, preferred_element_type=jnp.float32)

def solve_rows(system, targets):
    factor_lower = jnp.linalg.cholesky(system)
    return jax.scipy.linalg.cho_solve((factor_lower, True), targets.T).T

def add_rows(running, addition, start):
    previous = lax.dynamic_slice_in_dim(running, start, addition.shape[0], 0)
    return lax.dynamic_update_slice_in_dim(running, previous + addition, start, 0)

def mode_first(tiles, tile_list, orb_factor, nu_factor):

    def tile_step(running, tile_item):
        tile_block, coords = tile_item
        nu_block = lax.dynamic_slice_in_dim(nu_factor, (coords[2] * TILE).astype(jnp.int32), TILE, 0)
        orb_block = lax.dynamic_slice_in_dim(orb_factor, (coords[1] * TILE).astype(jnp.int32), TILE, 0)
        contracted = jnp.dot(tile_block.reshape(TILE * TILE, TILE).astype(jnp.float32), nu_block.astype(jnp.float32), precision=highest, preferred_element_type=jnp.float32).reshape(TILE, TILE, R)
        addition = lax.optimization_barrier(jnp.sum(contracted * orb_block[None], axis=1)) * coords[3].astype(jnp.float32)
        return (add_rows(running, addition, (coords[0] * TILE).astype(jnp.int32)), None)
    running, _ = lax.scan(tile_step, jnp.zeros((P_SIZE, R), jnp.float32), (tiles, tile_list.T))
    return running

def mode_second(tiles, tile_list, aux_factor, nu_factor):

    def tile_step(running, tile_item):
        tile_block, coords = tile_item
        nu_block = lax.dynamic_slice_in_dim(nu_factor, (coords[2] * TILE).astype(jnp.int32), TILE, 0)
        aux_block = lax.dynamic_slice_in_dim(aux_factor, (coords[0] * TILE).astype(jnp.int32), TILE, 0)
        contracted = jnp.dot(tile_block.reshape(TILE * TILE, TILE).astype(jnp.float32), nu_block.astype(jnp.float32), precision=highest, preferred_element_type=jnp.float32).reshape(TILE, TILE, R)
        addition = lax.optimization_barrier(jnp.sum(contracted * aux_block[:, None, :], axis=0)) * coords[3].astype(jnp.float32)
        return (add_rows(running, addition, (coords[1] * TILE).astype(jnp.int32)), None)
    running, _ = lax.scan(tile_step, jnp.zeros((MU, R), jnp.float32), (tiles, tile_list.T))
    return running

def mode_third(tiles, tile_list, aux_factor, orb_factor):

    def tile_step(running, tile_item):
        tile_block, coords = tile_item
        aux_block = lax.dynamic_slice_in_dim(aux_factor, (coords[0] * TILE).astype(jnp.int32), TILE, 0)
        orb_block = lax.dynamic_slice_in_dim(orb_factor, (coords[1] * TILE).astype(jnp.int32), TILE, 0)
        contracted = lax.dot_general(tile_block.astype(jnp.float32), aux_block.astype(jnp.float32), (((0,), (0,)), ((), ())), precision=highest, preferred_element_type=jnp.float32).reshape(TILE, TILE, R)
        addition = lax.optimization_barrier(jnp.sum(contracted * orb_block[:, None, :], axis=0)) * coords[3].astype(jnp.float32)
        return (add_rows(running, addition, (coords[2] * TILE).astype(jnp.int32)), None)
    running, _ = lax.scan(tile_step, jnp.zeros((NU, R), jnp.float32), (tiles, tile_list.T))
    return running

def normalize(values, row_count):
    scales = jnp.sqrt(lax.optimization_barrier(jnp.sum(values * values, axis=0)) / row_count + epsilon)
    scaled = values / scales
    return (scaled, gram_of(scaled) / row_count)

def reference(tiles, tile_list, orb_factor, nu_factor):
    identity = jnp.eye(R, dtype=jnp.float32)
    s_orb = gram_of(orb_factor) / MU
    s_nu = gram_of(nu_factor) / NU
    first_terms = mode_first(tiles, tile_list, orb_factor, nu_factor)
    a_new = solve_rows(s_orb * s_nu + ridge_weight * identity, first_terms)
    aux_factor, s_first = normalize(a_new, P_SIZE)
    second_terms = mode_second(tiles, tile_list, aux_factor, nu_factor)
    b_new = solve_rows(s_first * s_nu + ridge_weight * identity, second_terms)
    orb_updated, s_second = normalize(b_new, MU)
    third_terms = mode_third(tiles, tile_list, aux_factor, orb_updated)
    c_new = solve_rows(s_first * s_second + ridge_weight * identity, third_terms)
    nu_updated, _ = normalize(c_new, NU)
    return (aux_factor, orb_updated, nu_updated)
```

```python
import jax
import jax.numpy as jnp
from jax import lax
from jax.experimental import pallas as pl
from jax.experimental.pallas import tpu as pltpu
from jax.sharding import PartitionSpec as P

P_SIZE = 16384
MU = 4096
NU = 512
RANK = 256
EDGE = 64
SLOTS = 8
WIDE = 16
BLOCK = 32

ridge_weight = 0.5
epsilon = 1e-06
highest = lax.Precision.HIGHEST
f32 = jnp.float32
bf16 = jnp.bfloat16
params = pltpu.CompilerParams(vmem_limit_bytes=40 * 1024 * 1024)


def split(values):
    high = values.astype(bf16)
    return high, (values - high.astype(f32)).astype(bf16)


def weights_of(block):
    high, low = split(block)
    return jnp.concatenate([high, high, low], axis=0)


def dot32(left, right):
    return jnp.dot(left, right, precision=highest, preferred_element_type=f32)


def gram_of(matrix):
    return lax.dot_general(
        matrix, matrix, (((0,), (0,)), ((), ())), precision=highest, preferred_element_type=f32
    )


def rows_at(ref, tile_index):
    return ref[pl.ds(pl.multiple_of(tile_index * EDGE, EDGE), EDGE), :]


def first_kernel(list_ref, tile_ref, orb_ref, nu_ref, out_ref):
    slot = pl.program_id(0)

    @pl.when(slot == 0)
    def _():
        out_ref[...] = jnp.zeros_like(out_ref)

    @pl.when(list_ref[3, slot] > 0)
    def _():
        first = lax.rem(list_ref[0, slot], 8)
        second = lax.rem(list_ref[1, slot], 8)
        weights = weights_of(rows_at(nu_ref, list_ref[2, slot]))

        def part(index, total):
            at = pl.multiple_of(index * WIDE * EDGE, WIDE * EDGE)
            high, low = split(tile_ref[0, :, pl.ds(at, WIDE * EDGE)])
            stacked = []
            for j in range(WIDE):
                lanes = slice(j * EDGE, (j + 1) * EDGE)
                stacked.append(jnp.concatenate([high[:, lanes], low[:, lanes], high[:, lanes]], axis=1))
            product = jnp.dot(
                jnp.concatenate(stacked, axis=0), weights, preferred_element_type=f32
            ).reshape(WIDE, EDGE, RANK)
            orb_rows = orb_ref[pl.ds(pl.multiple_of(second * EDGE + index * WIDE, WIDE), WIDE), :]
            return total + jnp.sum(product * orb_rows[:, None, :], axis=0)

        total = lax.fori_loop(0, EDGE // WIDE, part, jnp.zeros((EDGE, RANK), f32))
        at = pl.ds(pl.multiple_of(first * EDGE, EDGE), EDGE)
        out_ref[at, :] = out_ref[at, :] + total


def contract_first(tile_ref, index, weights):
    at = pl.multiple_of(index * WIDE * EDGE, WIDE * EDGE)
    high, low = split(tile_ref[0, :, pl.ds(at, WIDE * EDGE)])
    return lax.dot_general(
        jnp.concatenate([high, low, high], axis=0),
        weights,
        (((0,), (0,)), ((), ())),
        preferred_element_type=f32,
    ).reshape(WIDE, EDGE, RANK)


def second_kernel(list_ref, tile_ref, aux_ref, nu_ref, out_ref):
    slot = pl.program_id(0)

    @pl.when(slot == 0)
    def _():
        out_ref[...] = jnp.zeros_like(out_ref)

    @pl.when(list_ref[3, slot] > 0)
    def _():
        second = lax.rem(list_ref[1, slot], 8)
        weights = weights_of(rows_at(aux_ref, lax.rem(list_ref[0, slot], 8)))
        nu_rows = rows_at(nu_ref, list_ref[2, slot])

        @pl.loop(0, EDGE // WIDE)
        def _(index):
            product = contract_first(tile_ref, index, weights)
            addition = jnp.sum(product * nu_rows[None], axis=1)
            at = pl.ds(pl.multiple_of(second * EDGE + index * WIDE, WIDE), WIDE)
            out_ref[at, :] = out_ref[at, :] + addition


def third_kernel(list_ref, tile_ref, aux_ref, orb_ref, out_ref):
    slot = pl.program_id(0)

    @pl.when(slot == 0)
    def _():
        out_ref[...] = jnp.zeros_like(out_ref)

    @pl.when(list_ref[3, slot] > 0)
    def _():
        second = lax.rem(list_ref[1, slot], 8)
        weights = weights_of(rows_at(aux_ref, lax.rem(list_ref[0, slot], 8)))

        def part(index, total):
            product = contract_first(tile_ref, index, weights)
            orb_rows = orb_ref[pl.ds(pl.multiple_of(second * EDGE + index * WIDE, WIDE), WIDE), :]
            return total + jnp.sum(product * orb_rows[:, None, :], axis=0)

        total = lax.fori_loop(0, EDGE // WIDE, part, jnp.zeros((EDGE, RANK), f32))
        at = pl.ds(pl.multiple_of(list_ref[2, slot] * EDGE, EDGE), EDGE)
        out_ref[at, :] = out_ref[at, :] + total


def live_slot(slot, list_ref):
    count = list_ref[3, 0]
    for other in range(1, SLOTS):
        count = count + list_ref[3, other]
    return jnp.maximum(jnp.minimum(slot, count - 1), 0)


def over_tiles(kernel, tile_list, tiles, left, right, name):
    whole = pl.BlockSpec((512, RANK), lambda slot, list_ref: (0, 0))
    return pl.pallas_call(
        kernel,
        out_shape=jax.ShapeDtypeStruct((512, RANK), f32),
        grid_spec=pltpu.PrefetchScalarGridSpec(
            num_scalar_prefetch=1,
            grid=(SLOTS,),
            in_specs=[
                pl.BlockSpec((1, EDGE, EDGE * EDGE), lambda slot, list_ref: (live_slot(slot, list_ref), 0, 0)),
                whole,
                whole,
            ],
            out_specs=whole,
        ),
        compiler_params=params,
        cost_estimate=pl.CostEstimate(flops=7 * 10**9, bytes_accessed=10**7, transcendentals=0),
        name=name,
    )(tile_list, tiles, left, right)


def sweep8(matrix):
    size = matrix.shape[0]
    panel = matrix[0:8, :]
    cell = {}
    for i in range(8):
        for j in range(i, 8):
            cell[i, j] = jnp.broadcast_to(panel[i : i + 1, j : j + 1], (8, size))
    get = lambda i, j: cell[min(i, j), max(i, j)]
    for k in range(8):
        pivot = 1.0 / get(k, k)
        scaled = {i: get(i, k) * pivot for i in range(8) if i != k}
        new = {}
        for i in range(8):
            for j in range(i, 8):
                if i != k and j != k:
                    new[i, j] = get(i, j) - scaled[i] * get(j, k)
        for i in range(8):
            if i != k:
                new[min(i, k), max(i, k)] = scaled[i]
        new[k, k] = -pivot
        cell = new
    lane = lax.broadcasted_iota(jnp.int32, (8, size), 1)
    sub = lax.broadcasted_iota(jnp.int32, (8, size), 0)
    marked = jnp.where(lane < 8, jnp.where(lane == sub, -1.0, 0.0), panel)
    result = jnp.zeros((8, size), f32)
    for j in range(8):
        column = get(7, j)
        for i in range(7):
            column = jnp.where(sub == i, get(i, j), column)
        result = result - column * jnp.broadcast_to(marked[j : j + 1, :], (8, size))
    row_id = lax.broadcasted_iota(jnp.int32, (size, size), 0)
    col_id = lax.broadcasted_iota(jnp.int32, (size, size), 1)
    kept = jnp.where((row_id < 8) | (col_id < 8), 0.0, matrix)
    left = jnp.where(row_id < 8, jnp.where(row_id == col_id, -1.0, 0.0), matrix)
    for j in range(8):
        kept = kept - jnp.broadcast_to(left[:, j : j + 1], (size, size)) * result[j : j + 1, :]
    kept = jnp.concatenate([kept[8:], kept[:8]], axis=0)
    return jnp.concatenate([kept[:, 8:], kept[:, :8]], axis=1)


def invert(work_ref):
    row_id = lax.broadcasted_iota(jnp.int32, (RANK, RANK), 0)
    col_id = lax.broadcasted_iota(jnp.int32, (RANK, RANK), 1)
    lead = (row_id < BLOCK) | (col_id < BLOCK)
    lane = lax.broadcasted_iota(jnp.int32, (BLOCK, RANK), 1)
    sub = lax.broadcasted_iota(jnp.int32, (BLOCK, RANK), 0)

    @pl.loop(0, RANK // BLOCK)
    def _(step):
        matrix = work_ref[...]
        small = matrix[:BLOCK, :BLOCK]
        for _ in range(BLOCK // 8):
            small = sweep8(small)
        marked = jnp.where(lane < BLOCK, jnp.where(lane == sub, -1.0, 0.0), matrix[:BLOCK, :])
        result = dot32(small, marked)
        update = lax.dot_general(
            marked, result, (((0,), (0,)), ((), ())), precision=highest, preferred_element_type=f32
        )
        kept = jnp.where(lead, 0.0, matrix) + update
        kept = jnp.concatenate([kept[BLOCK:], kept[:BLOCK]], axis=0)
        work_ref[...] = jnp.concatenate([kept[:, BLOCK:], kept[:, :BLOCK]], axis=1)

    work_ref[...] = -work_ref[...]


def scaled_gram(gram, count, scaled):
    if not scaled:
        return gram * (1.0 / count)
    row_id = lax.broadcasted_iota(jnp.int32, (RANK, RANK), 0)
    col_id = lax.broadcasted_iota(jnp.int32, (RANK, RANK), 1)
    squares = jnp.where(row_id == col_id, gram, 0.0)
    along = jnp.sqrt(jnp.sum(squares, axis=0, keepdims=True) * (1.0 / count) + epsilon)
    down = jnp.sqrt(jnp.sum(squares, axis=1, keepdims=True) * (1.0 / count) + epsilon)
    return gram / down / along * (1.0 / count)


def inverse_of(left, left_count, left_scaled, right, right_count, right_scaled, name):
    def kernel(left_ref, right_ref, out_ref):
        row_id = lax.broadcasted_iota(jnp.int32, (RANK, RANK), 0)
        col_id = lax.broadcasted_iota(jnp.int32, (RANK, RANK), 1)
        system = scaled_gram(left_ref[...], left_count, left_scaled) * scaled_gram(
            right_ref[...], right_count, right_scaled
        )
        out_ref[...] = system + jnp.where(row_id == col_id, ridge_weight, 0.0)
        invert(out_ref)

    return pl.pallas_call(
        kernel,
        out_shape=jax.ShapeDtypeStruct((RANK, RANK), f32),
        compiler_params=params,
        cost_estimate=pl.CostEstimate(flops=10 * 10**9, bytes_accessed=10**6, transcendentals=0),
        name=name,
    )(left, right)


def solve_and_gram(terms, inverse, divisor, name):
    def kernel(terms_ref, inverse_ref, divisor_ref, out_ref, gram_ref):
        out_ref[...] = dot32(terms_ref[...] / divisor_ref[...], inverse_ref[...])
        gram_ref[...] = gram_of(out_ref[...])

    return pl.pallas_call(
        kernel,
        out_shape=(jax.ShapeDtypeStruct((512, RANK), f32), jax.ShapeDtypeStruct((RANK, RANK), f32)),
        compiler_params=params,
        name=name,
    )(terms, inverse, divisor)


def exchange(pieces, axis):
    return lax.all_to_all(pieces, axis, 0, 0)


def spread(piece, axis):
    count = lax.axis_size(axis)
    return exchange(jnp.broadcast_to(piece[None], (count,) + piece.shape), axis)


def scale_of(gram, count):
    return jnp.sqrt(jnp.diagonal(gram) / count + epsilon)[None, :]


def per_device(tiles, tile_list, orb_factor, nu_factor):
    n_aux = lax.axis_size("aux")
    n_orb = lax.axis_size("orb")
    m_orb = 512 // n_orb
    m_aux = 512 // n_aux
    g_orb = RANK // n_orb
    g_aux = RANK // n_aux

    gram_nu = gram_of(nu_factor)
    gram_orb = gram_of(orb_factor)
    slab_orb = jnp.sum(exchange(gram_orb.reshape(n_orb, g_orb, RANK), "orb"), axis=0)
    partial_first = over_tiles(first_kernel, tile_list, tiles, orb_factor, nu_factor, "first_terms")
    received = exchange(
        jnp.concatenate(
            [
                partial_first.reshape(n_orb, m_orb, RANK),
                jnp.broadcast_to(slab_orb[None], (n_orb, g_orb, RANK)),
            ],
            axis=1,
        ),
        "orb",
    )
    gram_orb = received[:, m_orb:].reshape(RANK, RANK)
    first_terms = spread(jnp.sum(received[:, :m_orb], axis=0), "orb").reshape(512, RANK)
    inverse_first = inverse_of(gram_orb, MU, False, gram_nu, NU, False, "inverse_first")

    ones = jnp.ones((1, RANK), f32)
    a_new, gram_part = solve_and_gram(first_terms, inverse_first, ones, "solve_first")
    slab_aux = jnp.sum(exchange(gram_part.reshape(n_aux, g_aux, RANK), "aux"), axis=0)
    partial_second = over_tiles(second_kernel, tile_list, tiles, a_new, nu_factor, "second_terms")
    received = exchange(
        jnp.concatenate(
            [
                partial_second.reshape(n_aux, m_aux, RANK),
                jnp.broadcast_to(slab_aux[None], (n_aux, g_aux, RANK)),
            ],
            axis=1,
        ),
        "aux",
    )
    gram_aux = received[:, m_aux:].reshape(RANK, RANK)
    second_terms = spread(jnp.sum(received[:, :m_aux], axis=0), "aux").reshape(512, RANK)
    inverse_second = inverse_of(gram_aux, P_SIZE, True, gram_nu, NU, False, "inverse_second")
    scale_first = scale_of(gram_aux, P_SIZE)
    aux_factor = a_new / scale_first

    b_new, gram_part = solve_and_gram(second_terms, inverse_second, scale_first, "solve_second")
    slab = lax.dynamic_slice_in_dim(gram_part, lax.axis_index("aux") * g_aux, g_aux, 0)
    slab_orb = jnp.sum(spread(slab, "orb"), axis=0)
    partial_third = over_tiles(third_kernel, tile_list, tiles, a_new, b_new, "third_terms")
    received = exchange(
        jnp.concatenate(
            [
                partial_third.reshape(n_aux, m_aux, RANK),
                jnp.broadcast_to(slab_orb[None], (n_aux, g_aux, RANK)),
            ],
            axis=1,
        ),
        "aux",
    )
    gram_orb = received[:, m_aux:].reshape(RANK, RANK)
    piece = jnp.sum(spread(jnp.sum(received[:, :m_aux], axis=0), "orb"), axis=0)
    third_terms = spread(piece, "aux").reshape(512, RANK)
    inverse_third = inverse_of(gram_aux, P_SIZE, True, gram_orb, MU, True, "inverse_third")
    scale_second = scale_of(gram_orb, MU)
    orb_updated = b_new / scale_second

    c_new, gram_nu = solve_and_gram(third_terms, inverse_third, scale_first * scale_second, "solve_third")
    nu_updated = c_new / jnp.sqrt(jnp.sum(c_new * c_new, axis=0) / NU + epsilon)
    return (aux_factor, orb_updated, nu_updated)


def solution(mesh):
    return jax.shard_map(
        per_device,
        mesh=mesh,
        in_specs=(P(("aux", "orb"), None, None), P(None, ("aux", "orb")), P("orb", None), P()),
        out_specs=(P("aux", None), P("orb", None), P()),
        check_vma=False,
    )
```

```python
import jax
import jax.numpy as jnp
from jax import lax
from jax.experimental import pallas as pl
from jax.experimental.pallas import tpu as pltpu
from jax.sharding import PartitionSpec as P

P_SIZE = 16384
MU = 4096
NU = 512
RANK = 256
EDGE = 64
SLOTS = 8
WIDE = 16
BLOCK = 32

ridge_weight = 0.5
epsilon = 1e-06
highest = lax.Precision.HIGHEST
f32 = jnp.float32
bf16 = jnp.bfloat16
params = pltpu.CompilerParams(vmem_limit_bytes=60 * 1024 * 1024)


def split(values):
    high = values.astype(bf16)
    return high, (values - high.astype(f32)).astype(bf16)


def weights_of(block):
    high, low = split(block)
    return jnp.concatenate([high, high, low], axis=0)


def dot32(left, right):
    return jnp.dot(left, right, precision=highest, preferred_element_type=f32)


def gram_of(matrix):
    return lax.dot_general(
        matrix, matrix, (((0,), (0,)), ((), ())), precision=highest, preferred_element_type=f32
    )


def rows_at(ref, tile_index):
    return ref[pl.ds(pl.multiple_of(tile_index * EDGE, EDGE), EDGE), :]


def first_kernel(list_ref, tile_ref, orb_ref, nu_ref, out_ref):
    slot = pl.program_id(0)

    @pl.when(slot == 0)
    def _():
        out_ref[...] = jnp.zeros_like(out_ref)

    @pl.when(list_ref[3, slot] > 0)
    def _():
        first = lax.rem(list_ref[0, slot], 8)
        second = lax.rem(list_ref[1, slot], 8)
        weights = weights_of(rows_at(nu_ref, list_ref[2, slot]))

        def part(index, total):
            at = pl.multiple_of(index * WIDE * EDGE, WIDE * EDGE)
            high, low = split(tile_ref[0, :, pl.ds(at, WIDE * EDGE)])
            stacked = []
            for j in range(WIDE):
                lanes = slice(j * EDGE, (j + 1) * EDGE)
                stacked.append(jnp.concatenate([high[:, lanes], low[:, lanes], high[:, lanes]], axis=1))
            product = jnp.dot(
                jnp.concatenate(stacked, axis=0), weights, preferred_element_type=f32
            ).reshape(WIDE, EDGE, RANK)
            orb_rows = orb_ref[pl.ds(pl.multiple_of(second * EDGE + index * WIDE, WIDE), WIDE), :]
            return total + jnp.sum(product * orb_rows[:, None, :], axis=0)

        total = lax.fori_loop(0, EDGE // WIDE, part, jnp.zeros((EDGE, RANK), f32), unroll=True)
        at = pl.ds(pl.multiple_of(first * EDGE, EDGE), EDGE)
        out_ref[at, :] = out_ref[at, :] + total


def contract_first(tile_ref, index, weights):
    at = pl.multiple_of(index * WIDE * EDGE, WIDE * EDGE)
    high, low = split(tile_ref[0, :, pl.ds(at, WIDE * EDGE)])
    return lax.dot_general(
        jnp.concatenate([high, low, high], axis=0),
        weights,
        (((0,), (0,)), ((), ())),
        preferred_element_type=f32,
    ).reshape(WIDE, EDGE, RANK)


def second_kernel(list_ref, tile_ref, aux_ref, nu_ref, out_ref):
    slot = pl.program_id(0)

    @pl.when(slot == 0)
    def _():
        out_ref[...] = jnp.zeros_like(out_ref)

    @pl.when(list_ref[3, slot] > 0)
    def _():
        second = lax.rem(list_ref[1, slot], 8)
        weights = weights_of(rows_at(aux_ref, lax.rem(list_ref[0, slot], 8)))
        nu_rows = rows_at(nu_ref, list_ref[2, slot])

        @pl.loop(0, EDGE // WIDE, unroll=True)
        def _(index):
            product = contract_first(tile_ref, index, weights)
            addition = jnp.sum(product * nu_rows[None], axis=1)
            at = pl.ds(pl.multiple_of(second * EDGE + index * WIDE, WIDE), WIDE)
            out_ref[at, :] = out_ref[at, :] + addition


def third_kernel(list_ref, tile_ref, aux_ref, orb_ref, out_ref):
    slot = pl.program_id(0)

    @pl.when(slot == 0)
    def _():
        out_ref[...] = jnp.zeros_like(out_ref)

    @pl.when(list_ref[3, slot] > 0)
    def _():
        second = lax.rem(list_ref[1, slot], 8)
        weights = weights_of(rows_at(aux_ref, lax.rem(list_ref[0, slot], 8)))

        def part(index, total):
            product = contract_first(tile_ref, index, weights)
            orb_rows = orb_ref[pl.ds(pl.multiple_of(second * EDGE + index * WIDE, WIDE), WIDE), :]
            return total + jnp.sum(product * orb_rows[:, None, :], axis=0)

        total = lax.fori_loop(0, EDGE // WIDE, part, jnp.zeros((EDGE, RANK), f32), unroll=True)
        at = pl.ds(pl.multiple_of(list_ref[2, slot] * EDGE, EDGE), EDGE)
        out_ref[at, :] = out_ref[at, :] + total


def live_slot(slot, list_ref):
    count = list_ref[3, 0]
    for other in range(1, SLOTS):
        count = count + list_ref[3, other]
    return jnp.maximum(jnp.minimum(slot, count - 1), 0)


def over_tiles(kernel, tile_list, tiles, left, right):
    entire = pl.BlockSpec((512, RANK), lambda slot, list_ref: (0, 0))
    return pl.pallas_call(
        kernel,
        out_shape=jax.ShapeDtypeStruct((512, RANK), f32),
        grid_spec=pltpu.PrefetchScalarGridSpec(
            num_scalar_prefetch=1,
            grid=(SLOTS,),
            in_specs=[
                pl.BlockSpec((1, EDGE, EDGE * EDGE), lambda slot, list_ref: (live_slot(slot, list_ref), 0, 0)),
                entire,
                entire,
            ],
            out_specs=entire,
        ),
        compiler_params=params,
        cost_estimate=pl.CostEstimate(flops=7 * 10**9, bytes_accessed=10**7, transcendentals=0),
        name=kernel.__name__.removesuffix("_kernel") + "_terms",
    )(tile_list, tiles, left, right)


def tree_sum(terms):
    terms = list(terms)
    while len(terms) > 1:
        terms = [sum(terms[i + 1 : i + 2], terms[i]) for i in range(0, len(terms), 2)]
    return terms[0]


def invert_cells(cell):
    def get(i, j):
        return cell[min(i, j), max(i, j)]

    for k in range(0, 8, 2):
        pivots = (k, k + 1)
        others = [i for i in range(8) if i not in pivots]
        top, cross, low = cell[k, k], cell[k, k + 1], cell[k + 1, k + 1]
        factor = 1.0 / (top * low - cross * cross)
        top, cross, low = low * factor, -cross * factor, top * factor
        pair = {
            i: (get(i, k) * top + get(i, k + 1) * cross, get(i, k) * cross + get(i, k + 1) * low)
            for i in others
        }
        fresh = {}
        for i in others:
            for j in others:
                if i <= j:
                    fresh[i, j] = cell[i, j] - pair[i][0] * get(j, k) - pair[i][1] * get(j, k + 1)
            for pivot, value in zip(pivots, pair[i]):
                fresh[min(i, pivot), max(i, pivot)] = value
        fresh[k, k], fresh[k, k + 1], fresh[k + 1, k + 1] = -top, -cross, -low
        cell = fresh
    return cell


def sweep8(matrix, at):
    rows = slice(at, at + 8)
    panel = matrix[rows, :]
    columns = [jnp.broadcast_to(panel[:, at + j : at + j + 1], (8, BLOCK)) for j in range(8)]
    cell = invert_cells(
        {
            (i, j): jnp.broadcast_to(columns[j][i : i + 1, :], (8, BLOCK))
            for i in range(8)
            for j in range(i, 8)
        }
    )
    lane = lax.broadcasted_iota(jnp.int32, (8, BLOCK), 1)
    sub = lax.broadcasted_iota(jnp.int32, (8, BLOCK), 0)
    marked = jnp.where((lane >= at) & (lane < at + 8), jnp.where(lane == sub + at, -1.0, 0.0), panel)
    lines = [jnp.broadcast_to(marked[j : j + 1, :], (8, BLOCK)) for j in range(8)]
    result = [tree_sum(cell[min(i, j), max(i, j)] * lines[j] for j in range(8)) for i in range(8)]
    row_id = lax.broadcasted_iota(jnp.int32, (BLOCK, BLOCK), 0)
    col_id = lax.broadcasted_iota(jnp.int32, (BLOCK, BLOCK), 1)
    in_rows = (row_id >= at) & (row_id < at + 8)
    in_columns = (col_id >= at) & (col_id < at + 8)
    kept = jnp.where(in_rows | in_columns, 0.0, matrix)
    left = jnp.where(in_rows, jnp.where(row_id == col_id, -1.0, 0.0), matrix)
    spreads = [jnp.broadcast_to(left[:, at + j : at + j + 1], (BLOCK, BLOCK)) for j in range(8)]
    parts = []
    for first in range(0, BLOCK, 8):
        group = slice(first, first + 8)
        parts.append(kept[group] + tree_sum(spreads[i][group] * result[i] for i in range(8)))
    return jnp.concatenate(parts, axis=0)


def split3(values):
    high = values.astype(bf16)
    rest = values - high.astype(f32)
    middle = rest.astype(bf16)
    return high, middle, (rest - middle.astype(f32)).astype(bf16)


def invert(matrix):
    row_id = lax.broadcasted_iota(jnp.int32, (RANK, RANK), 0)
    col_id = lax.broadcasted_iota(jnp.int32, (RANK, RANK), 1)
    lane = lax.broadcasted_iota(jnp.int32, (BLOCK, RANK), 1)
    sub = lax.broadcasted_iota(jnp.int32, (BLOCK, RANK), 0)
    for at in range(0, RANK, BLOCK):
        panel = matrix[at : at + BLOCK, :]
        small = panel[:, at : at + BLOCK]
        marked = jnp.where((lane >= at) & (lane < at + BLOCK), jnp.where(lane == sub + at, -1.0, 0.0), panel)
        a, b, c = split3(marked)
        for step in range(0, BLOCK, 8):
            small = sweep8(small, step)
        p, q, r = split3(small)
        result = jnp.dot(
            jnp.concatenate([p, p, q, p, r, q], axis=1),
            jnp.concatenate([a, b, a, c, a, b], axis=0),
            preferred_element_type=f32,
        )
        d, e, f = split3(result)
        update = lax.dot_general(
            jnp.concatenate([a, a, b, a, c, b], axis=0),
            jnp.concatenate([d, e, d, f, d, e], axis=0),
            (((0,), (0,)), ((), ())),
            preferred_element_type=f32,
        )
        in_block = (row_id >= at) & (row_id < at + BLOCK) | (col_id >= at) & (col_id < at + BLOCK)
        matrix = jnp.where(in_block, 0.0, matrix) + update
    return -matrix


HALF = RANK // 2
PACKED = jax.ShapeDtypeStruct((HALF + HALF // 2, RANK), f32)
SQUARE = jax.ShapeDtypeStruct((RANK, RANK), f32)
ROWS = jax.ShapeDtypeStruct((512, RANK), f32)
LINE = jax.ShapeDtypeStruct((1, RANK), f32)


def pack(gram):
    corner = gram[HALF:, HALF:]
    corner = jnp.concatenate([corner[: HALF // 2], corner[HALF // 2 :]], axis=1)
    return jnp.concatenate([gram[:HALF], corner], axis=0)


def unpack(packed):
    corner = packed[HALF:]
    corner = jnp.concatenate([corner[:, :HALF], corner[:, HALF:]], axis=0)
    below = jnp.concatenate([packed[:HALF, HALF:].T, corner], axis=1)
    return jnp.concatenate([packed[:HALF], below], axis=0)


def scales(gram, count, axis):
    row_id = lax.broadcasted_iota(jnp.int32, (RANK, RANK), 0)
    col_id = lax.broadcasted_iota(jnp.int32, (RANK, RANK), 1)
    squares = jnp.sum(jnp.where(row_id == col_id, gram, 0.0), axis=axis, keepdims=True)
    return jnp.sqrt(squares * (1.0 / count) + epsilon)


def scaled_gram(gram, count):
    return gram / scales(gram, count, 1) / scales(gram, count, 0) * (1.0 / count)


def system_inverse(left, right):
    row_id = lax.broadcasted_iota(jnp.int32, (RANK, RANK), 0)
    col_id = lax.broadcasted_iota(jnp.int32, (RANK, RANK), 1)
    return invert(left * right + jnp.where(row_id == col_id, ridge_weight, 0.0))


def inverse_first_kernel(orb_ref, nu_ref, out_ref):
    out_ref[...] = system_inverse(
        unpack(orb_ref[...]) * (1.0 / MU), gram_of(nu_ref[...]) * (1.0 / NU)
    )


def inverse_second_kernel(aux_ref, nu_ref, out_ref, scale_ref):
    scale_ref[...] = scales(aux_ref[...], P_SIZE, 0)
    out_ref[...] = system_inverse(
        scaled_gram(aux_ref[...], P_SIZE), gram_of(nu_ref[...]) * (1.0 / NU)
    )


def inverse_third_kernel(aux_ref, orb_ref, out_ref, scale_ref, both_ref):
    gram_orb = unpack(orb_ref[...])
    scale_ref[...] = scales(gram_orb, MU, 0)
    both_ref[...] = scales(gram_orb, MU, 0) * scales(aux_ref[...], P_SIZE, 0)
    out_ref[...] = system_inverse(scaled_gram(aux_ref[...], P_SIZE), scaled_gram(gram_orb, MU))


def gram_kernel(rows_ref, gram_ref):
    gram_ref[...] = pack(gram_of(rows_ref[...]))


def solve_first_kernel(terms_ref, inverse_ref, out_ref, gram_ref):
    out_ref[...] = dot32(terms_ref[...], inverse_ref[...])
    gram_ref[...] = gram_of(out_ref[...])


def solve_second_kernel(terms_ref, inverse_ref, scale_ref, out_ref, gram_ref):
    out_ref[...] = dot32(terms_ref[...] / scale_ref[...], inverse_ref[...])
    gram_ref[...] = pack(gram_of(out_ref[...]))


def solve_third_kernel(terms_ref, inverse_ref, scale_ref, out_ref):
    values = dot32(terms_ref[...] / scale_ref[...], inverse_ref[...])
    squares = jnp.sum(values * values, axis=0, keepdims=True)
    out_ref[...] = values / jnp.sqrt(squares * (1.0 / NU) + epsilon)


def whole(kernel, out_shape, *operands, flops=10**9):
    return pl.pallas_call(
        kernel,
        out_shape=out_shape,
        compiler_params=params,
        cost_estimate=pl.CostEstimate(flops=flops, bytes_accessed=10**6, transcendentals=0),
        name=kernel.__name__.removesuffix("_kernel"),
    )(*operands)


def exchange(pieces, axis):
    return lax.all_to_all(pieces, axis, 0, 0)


def spread(piece, axis):
    count = lax.axis_size(axis)
    return exchange(jnp.broadcast_to(piece[None], (count,) + piece.shape), axis)


def per_device(tiles, tile_list, orb_factor, nu_factor):
    n_aux = lax.axis_size("aux")
    n_orb = lax.axis_size("orb")
    m_orb = 512 // n_orb
    m_aux = 512 // n_aux
    g_aux = RANK // n_aux

    gram_orb = lax.psum(whole(gram_kernel, PACKED, orb_factor), "orb")
    partial_first = over_tiles(first_kernel, tile_list, tiles, orb_factor, nu_factor)
    received = exchange(partial_first.reshape(n_orb, m_orb, RANK), "orb")
    first_terms = spread(jnp.sum(received, axis=0), "orb").reshape(512, RANK)
    inverse_first = whole(inverse_first_kernel, SQUARE, gram_orb, nu_factor, flops=10**10)

    a_new, gram_part = whole(solve_first_kernel, (ROWS, SQUARE), first_terms, inverse_first)
    slab_aux = jnp.sum(exchange(gram_part.reshape(n_aux, g_aux, RANK), "aux"), axis=0)
    partial_second = over_tiles(second_kernel, tile_list, tiles, a_new, nu_factor)
    received = exchange(
        jnp.concatenate(
            [
                partial_second.reshape(n_aux, m_aux, RANK),
                jnp.broadcast_to(slab_aux[None], (n_aux, g_aux, RANK)),
            ],
            axis=1,
        ),
        "aux",
    )
    gram_aux = received[:, m_aux:].reshape(RANK, RANK)
    second_terms = spread(jnp.sum(received[:, :m_aux], axis=0), "aux").reshape(512, RANK)
    inverse_second, scale_first = whole(
        inverse_second_kernel, (SQUARE, LINE), gram_aux, nu_factor, flops=10**10
    )

    b_new, gram_part = whole(
        solve_second_kernel, (ROWS, PACKED), second_terms, inverse_second, scale_first
    )
    gram_orb = lax.psum(gram_part, "orb")
    partial_third = over_tiles(third_kernel, tile_list, tiles, a_new, b_new)
    received = exchange(partial_third.reshape(n_aux, m_aux, RANK), "aux")
    piece = jnp.sum(spread(jnp.sum(received, axis=0), "orb"), axis=0)
    third_terms = spread(piece, "aux").reshape(512, RANK)
    inverse_third, scale_second, scale_both = whole(
        inverse_third_kernel, (SQUARE, LINE, LINE), gram_aux, gram_orb, flops=10**10
    )
    nu_updated = whole(solve_third_kernel, ROWS, third_terms, inverse_third, scale_both)
    return (a_new / scale_first, b_new / scale_second, nu_updated)


def solution(mesh):
    return jax.shard_map(
        per_device,
        mesh=mesh,
        in_specs=(P(("aux", "orb"), None, None), P(None, ("aux", "orb")), P("orb", None), P()),
        out_specs=(P("aux", None), P("orb", None), P()),
        check_vma=False,
    )
```

```python
import jax
import jax.numpy as jnp
from jax import lax
from jax.experimental import pallas as pl
from jax.experimental.pallas import tpu as pltpu
from jax.sharding import PartitionSpec as P

P_SIZE = 16384
MU = 4096
NU = 512
RANK = 256
EDGE = 64
SLOTS = 8
WIDE = 16
BLOCK = 32

ridge_weight = 0.5
epsilon = 1e-06
f32 = jnp.float32
bf16 = jnp.bfloat16
params = pltpu.CompilerParams(vmem_limit_bytes=32 * 1024 * 1024)
tile_params = pltpu.CompilerParams(vmem_limit_bytes=57 * 1024 * 1024)


def split(values):
    high = values.astype(bf16)
    return high, (values - high.astype(f32)).astype(bf16)


def weights_of(block):
    high, low = split(block)
    return jnp.concatenate([high, high, low], axis=0)


def split3(values):
    high = values.astype(bf16)
    rest = values - high.astype(f32)
    middle = rest.astype(bf16)
    return high, middle, (rest - middle.astype(f32)).astype(bf16)


def stack_left(values, axis):
    high, middle, low = split3(values)
    return jnp.concatenate([high, high, middle, high, low, middle], axis=axis)


def stack_right(values):
    high, middle, low = split3(values)
    return jnp.concatenate([high, middle, high, low, high, middle], axis=0)


def dot32(left, right):
    return jnp.dot(stack_left(left, 1), stack_right(right), preferred_element_type=f32)


def gram_of(matrix):
    return lax.dot_general(
        stack_left(matrix, 0),
        stack_right(matrix),
        (((0,), (0,)), ((), ())),
        preferred_element_type=f32,
    )


def rows_at(ref, tile_index):
    return ref[pl.ds(pl.multiple_of(tile_index * EDGE, EDGE), EDGE), :]


def first_kernel(list_ref, tile_ref, orb_ref, nu_ref, out_ref):
    slot = pl.program_id(0)

    @pl.when(slot == 0)
    def _():
        out_ref[...] = jnp.zeros_like(out_ref)

    @pl.when(list_ref[3, slot] > 0)
    def _():
        first = lax.rem(list_ref[0, slot], 8)
        second = lax.rem(list_ref[1, slot], 8)
        weights = weights_of(rows_at(nu_ref, list_ref[2, slot]))

        def part(index, total):
            at = pl.multiple_of(index * WIDE * EDGE, WIDE * EDGE)
            high, low = split(tile_ref[0, :, pl.ds(at, WIDE * EDGE)])
            stacked = []
            for j in range(WIDE):
                lanes = slice(j * EDGE, (j + 1) * EDGE)
                stacked.append(jnp.concatenate([high[:, lanes], low[:, lanes], high[:, lanes]], axis=1))
            product = jnp.dot(
                jnp.concatenate(stacked, axis=0), weights, preferred_element_type=f32
            ).reshape(WIDE, EDGE, RANK)
            orb_rows = orb_ref[pl.ds(pl.multiple_of(second * EDGE + index * WIDE, WIDE), WIDE), :]
            return total + jnp.sum(product * orb_rows[:, None, :], axis=0)

        total = lax.fori_loop(0, EDGE // WIDE, part, jnp.zeros((EDGE, RANK), f32), unroll=True)
        at = pl.ds(pl.multiple_of(first * EDGE, EDGE), EDGE)
        out_ref[at, :] = out_ref[at, :] + total


def contract_first(tile_ref, index, weights):
    at = pl.multiple_of(index * WIDE * EDGE, WIDE * EDGE)
    high, low = split(tile_ref[0, :, pl.ds(at, WIDE * EDGE)])
    return lax.dot_general(
        jnp.concatenate([high, low, high], axis=0),
        weights,
        (((0,), (0,)), ((), ())),
        preferred_element_type=f32,
    ).reshape(WIDE, EDGE, RANK)


def second_kernel(list_ref, tile_ref, aux_ref, nu_ref, out_ref):
    slot = pl.program_id(0)

    @pl.when(slot == 0)
    def _():
        out_ref[...] = jnp.zeros_like(out_ref)

    @pl.when(list_ref[3, slot] > 0)
    def _():
        second = lax.rem(list_ref[1, slot], 8)
        weights = weights_of(rows_at(aux_ref, lax.rem(list_ref[0, slot], 8)))
        nu_rows = rows_at(nu_ref, list_ref[2, slot])

        @pl.loop(0, EDGE // WIDE, unroll=True)
        def _(index):
            product = contract_first(tile_ref, index, weights)
            addition = jnp.sum(product * nu_rows[None], axis=1)
            at = pl.ds(pl.multiple_of(second * EDGE + index * WIDE, WIDE), WIDE)
            out_ref[at, :] = out_ref[at, :] + addition


def third_kernel(list_ref, tile_ref, aux_ref, orb_ref, out_ref):
    slot = pl.program_id(0)

    @pl.when(slot == 0)
    def _():
        out_ref[...] = jnp.zeros_like(out_ref)

    @pl.when(list_ref[3, slot] > 0)
    def _():
        second = lax.rem(list_ref[1, slot], 8)
        weights = weights_of(rows_at(aux_ref, lax.rem(list_ref[0, slot], 8)))

        def part(index, total):
            product = contract_first(tile_ref, index, weights)
            orb_rows = orb_ref[pl.ds(pl.multiple_of(second * EDGE + index * WIDE, WIDE), WIDE), :]
            return total + jnp.sum(product * orb_rows[:, None, :], axis=0)

        total = lax.fori_loop(0, EDGE // WIDE, part, jnp.zeros((EDGE, RANK), f32), unroll=True)
        at = pl.ds(pl.multiple_of(list_ref[2, slot] * EDGE, EDGE), EDGE)
        out_ref[at, :] = out_ref[at, :] + total


def live_slot(slot, list_ref):
    count = list_ref[3, 0]
    for other in range(1, SLOTS):
        count = count + list_ref[3, other]
    return jnp.maximum(jnp.minimum(slot, count - 1), 0)


def over_tiles(kernel, tile_list, tiles, left, right):
    entire = pl.BlockSpec((512, RANK), lambda slot, list_ref: (0, 0))
    return pl.pallas_call(
        kernel,
        out_shape=jax.ShapeDtypeStruct((512, RANK), f32),
        grid_spec=pltpu.PrefetchScalarGridSpec(
            num_scalar_prefetch=1,
            grid=(SLOTS,),
            in_specs=[
                pl.BlockSpec((1, EDGE, EDGE * EDGE), lambda slot, list_ref: (live_slot(slot, list_ref), 0, 0)),
                entire,
                entire,
            ],
            out_specs=entire,
        ),
        compiler_params=tile_params,
        cost_estimate=pl.CostEstimate(flops=7 * 10**9, bytes_accessed=10**7, transcendentals=0),
        name=kernel.__name__.removesuffix("_kernel") + "_terms",
    )(tile_list, tiles, left, right)


def tree_sum(terms):
    terms = list(terms)
    while len(terms) > 1:
        terms = [sum(terms[i + 1 : i + 2], terms[i]) for i in range(0, len(terms), 2)]
    return terms[0]


def invert_cells(cell):
    def get(i, j):
        return cell[min(i, j), max(i, j)]

    for k in range(0, 8, 2):
        pivots = (k, k + 1)
        others = [i for i in range(8) if i not in pivots]
        top, cross, low = cell[k, k], cell[k, k + 1], cell[k + 1, k + 1]
        factor = 1.0 / (top * low - cross * cross)
        top, cross, low = low * factor, -cross * factor, top * factor
        pair = {
            i: (get(i, k) * top + get(i, k + 1) * cross, get(i, k) * cross + get(i, k + 1) * low)
            for i in others
        }
        fresh = {}
        for i in others:
            for j in others:
                if i <= j:
                    fresh[i, j] = cell[i, j] - pair[i][0] * get(j, k) - pair[i][1] * get(j, k + 1)
            for pivot, value in zip(pivots, pair[i]):
                fresh[min(i, pivot), max(i, pivot)] = value
        fresh[k, k], fresh[k, k + 1], fresh[k + 1, k + 1] = -top, -cross, -low
        cell = fresh
    return cell


def sweep8(matrix, at):
    rows = slice(at, at + 8)
    panel = matrix[rows, :]
    columns = [jnp.broadcast_to(panel[:, at + j : at + j + 1], (8, BLOCK)) for j in range(8)]
    cell = invert_cells(
        {
            (i, j): jnp.broadcast_to(columns[j][i : i + 1, :], (8, BLOCK))
            for i in range(8)
            for j in range(i, 8)
        }
    )
    lane = lax.broadcasted_iota(jnp.int32, (8, BLOCK), 1)
    sub = lax.broadcasted_iota(jnp.int32, (8, BLOCK), 0)
    marked = jnp.where((lane >= at) & (lane < at + 8), jnp.where(lane == sub + at, -1.0, 0.0), panel)
    lines = [jnp.broadcast_to(marked[j : j + 1, :], (8, BLOCK)) for j in range(8)]
    result = [tree_sum(cell[min(i, j), max(i, j)] * lines[j] for j in range(8)) for i in range(8)]
    row_id = lax.broadcasted_iota(jnp.int32, (BLOCK, BLOCK), 0)
    col_id = lax.broadcasted_iota(jnp.int32, (BLOCK, BLOCK), 1)
    in_rows = (row_id >= at) & (row_id < at + 8)
    in_columns = (col_id >= at) & (col_id < at + 8)
    kept = jnp.where(in_rows | in_columns, 0.0, matrix)
    left = jnp.where(in_rows, jnp.where(row_id == col_id, -1.0, 0.0), matrix)
    spreads = [jnp.broadcast_to(left[:, at + j : at + j + 1], (BLOCK, BLOCK)) for j in range(8)]
    parts = []
    for first in range(0, BLOCK, 8):
        group = slice(first, first + 8)
        parts.append(kept[group] + tree_sum(spreads[i][group] * result[i] for i in range(8)))
    return jnp.concatenate(parts, axis=0)


def sweep_blocks(matrix, first, last):
    row_id = lax.broadcasted_iota(jnp.int32, (RANK, RANK), 0)
    col_id = lax.broadcasted_iota(jnp.int32, (RANK, RANK), 1)
    lane = lax.broadcasted_iota(jnp.int32, (BLOCK, RANK), 1)
    sub = lax.broadcasted_iota(jnp.int32, (BLOCK, RANK), 0)
    for at in range(first, last, BLOCK):
        panel = matrix[at : at + BLOCK, :]
        small = panel[:, at : at + BLOCK]
        marked = jnp.where((lane >= at) & (lane < at + BLOCK), jnp.where(lane == sub + at, -1.0, 0.0), panel)
        for step in range(0, BLOCK, 8):
            small = sweep8(small, step)
        result = dot32(small, marked)
        update = lax.dot_general(
            stack_left(marked, 0),
            stack_right(result),
            (((0,), (0,)), ((), ())),
            preferred_element_type=f32,
        )
        in_block = (row_id >= at) & (row_id < at + BLOCK) | (col_id >= at) & (col_id < at + BLOCK)
        matrix = jnp.where(in_block, 0.0, matrix) + update
    return matrix


HALF = RANK // 2
PACKED = jax.ShapeDtypeStruct((HALF + HALF // 2, RANK), f32)
SQUARE = jax.ShapeDtypeStruct((RANK, RANK), f32)
ROWS = jax.ShapeDtypeStruct((512, RANK), f32)
LINE = jax.ShapeDtypeStruct((1, RANK), f32)


def pack(gram):
    corner = gram[HALF:, HALF:]
    corner = jnp.concatenate([corner[: HALF // 2], corner[HALF // 2 :]], axis=1)
    return jnp.concatenate([gram[:HALF], corner], axis=0)


def unpack(packed):
    corner = packed[HALF:]
    corner = jnp.concatenate([corner[:, :HALF], corner[:, HALF:]], axis=0)
    below = jnp.concatenate([packed[:HALF, HALF:].T, corner], axis=1)
    return jnp.concatenate([packed[:HALF], below], axis=0)


def scales(gram, count, axis):
    row_id = lax.broadcasted_iota(jnp.int32, (RANK, RANK), 0)
    col_id = lax.broadcasted_iota(jnp.int32, (RANK, RANK), 1)
    squares = jnp.sum(jnp.where(row_id == col_id, gram, 0.0), axis=axis, keepdims=True)
    return jnp.sqrt(squares * (1.0 / count) + epsilon)


def scaled_gram(gram, count):
    return gram / scales(gram, count, 1) / scales(gram, count, 0) * (1.0 / count)


def system_of(left, right):
    row_id = lax.broadcasted_iota(jnp.int32, (RANK, RANK), 0)
    col_id = lax.broadcasted_iota(jnp.int32, (RANK, RANK), 1)
    return left * right + jnp.where(row_id == col_id, ridge_weight, 0.0)


def inverse_first_kernel(orb_ref, nu_ref, out_ref):
    system = system_of(unpack(orb_ref[...]) * (1.0 / MU), nu_ref[...] * (1.0 / NU))
    out_ref[...] = -sweep_blocks(system, 0, RANK)


def inverse_second_kernel(aux_ref, nu_ref, out_ref, scale_ref):
    scale_ref[...] = scales(aux_ref[...], P_SIZE, 0)
    system = system_of(scaled_gram(aux_ref[...], P_SIZE), nu_ref[...] * (1.0 / NU))
    out_ref[...] = -sweep_blocks(system, 0, RANK)


def half_third_kernel(aux_ref, orb_ref, out_ref, scale_ref, both_ref):
    scale_ref[...] = scales(orb_ref[...], MU, 0)
    both_ref[...] = scales(orb_ref[...], MU, 0) * scales(aux_ref[...], P_SIZE, 0)
    system = system_of(scaled_gram(aux_ref[...], P_SIZE), scaled_gram(orb_ref[...], MU))
    out_ref[...] = sweep_blocks(system, 0, HALF)


def inverse_third_kernel(half_ref, out_ref):
    out_ref[...] = -sweep_blocks(half_ref[...], HALF, RANK)


def packed_gram_kernel(rows_ref, gram_ref):
    gram_ref[...] = pack(gram_of(rows_ref[...]))


def gram_kernel(rows_ref, gram_ref):
    gram_ref[...] = gram_of(rows_ref[...])


def solve_first_kernel(terms_ref, inverse_ref, out_ref, gram_ref):
    out_ref[...] = dot32(terms_ref[...], inverse_ref[...])
    gram_ref[...] = gram_of(out_ref[...])


def solve_second_kernel(terms_ref, inverse_ref, scale_ref, out_ref, gram_ref):
    out_ref[...] = dot32(terms_ref[...] / scale_ref[...], inverse_ref[...])
    gram_ref[...] = gram_of(out_ref[...])


def solve_third_kernel(terms_ref, inverse_ref, scale_ref, out_ref):
    values = dot32(terms_ref[...] / scale_ref[...], inverse_ref[...])
    squares = jnp.sum(values * values, axis=0, keepdims=True)
    out_ref[...] = values / jnp.sqrt(squares * (1.0 / NU) + epsilon)


def whole(kernel, out_shape, *operands, flops=10**9):
    return pl.pallas_call(
        kernel,
        out_shape=out_shape,
        compiler_params=params,
        cost_estimate=pl.CostEstimate(flops=flops, bytes_accessed=10**6, transcendentals=0),
        name=kernel.__name__.removesuffix("_kernel"),
    )(*operands)


def exchange(pieces, axis):
    return lax.all_to_all(pieces, axis, 0, 0)


def spread(piece, axis):
    count = lax.axis_size(axis)
    return exchange(jnp.broadcast_to(piece[None], (count,) + piece.shape), axis)


def beside(rows, slab):
    return jnp.concatenate([rows, jnp.broadcast_to(slab[None], rows.shape[:1] + slab.shape)], axis=1)


def per_device(tiles, tile_list, orb_factor, nu_factor):
    n_aux = lax.axis_size("aux")
    n_orb = lax.axis_size("orb")
    m_orb = 512 // n_orb
    m_aux = 512 // n_aux
    g_aux = RANK // n_aux

    gram_orb = whole(packed_gram_kernel, PACKED, orb_factor).reshape(n_orb, -1, RANK)
    slab_orb = jnp.sum(exchange(gram_orb, "orb"), axis=0)
    partial_first = over_tiles(first_kernel, tile_list, tiles, orb_factor, nu_factor)
    received = exchange(beside(partial_first.reshape(n_orb, m_orb, RANK), slab_orb), "orb")
    nu_later, _ = lax.optimization_barrier((nu_factor, partial_first))
    gram_nu = whole(gram_kernel, SQUARE, nu_later)
    gram_orb = received[:, m_orb:].reshape(PACKED.shape)
    first_terms = spread(jnp.sum(received[:, :m_orb], axis=0), "orb").reshape(512, RANK)
    inverse_first = whole(inverse_first_kernel, SQUARE, gram_orb, gram_nu, flops=10**10)

    a_new, gram_part = whole(solve_first_kernel, (ROWS, SQUARE), first_terms, inverse_first)
    slab_aux = jnp.sum(exchange(gram_part.reshape(n_aux, g_aux, RANK), "aux"), axis=0)
    partial_second = over_tiles(second_kernel, tile_list, tiles, a_new, nu_factor)
    received = exchange(beside(partial_second.reshape(n_aux, m_aux, RANK), slab_aux), "aux")
    gram_aux = received[:, m_aux:].reshape(RANK, RANK)
    second_terms = spread(jnp.sum(received[:, :m_aux], axis=0), "aux").reshape(512, RANK)
    inverse_second, scale_first = whole(
        inverse_second_kernel, (SQUARE, LINE), gram_aux, gram_nu, flops=10**10
    )

    b_new, gram_part = whole(
        solve_second_kernel, (ROWS, SQUARE), second_terms, inverse_second, scale_first
    )
    slab = lax.dynamic_slice_in_dim(gram_part, lax.axis_index("aux") * g_aux, g_aux, 0)
    slab_orb = jnp.sum(spread(slab, "orb"), axis=0)
    partial_third = over_tiles(third_kernel, tile_list, tiles, a_new, b_new)
    received = exchange(beside(partial_third.reshape(n_aux, m_aux, RANK), slab_orb), "aux")
    gram_orb = received[:, m_aux:].reshape(RANK, RANK)
    half, scale_second, scale_both = whole(
        half_third_kernel, (SQUARE, LINE, LINE), gram_aux, gram_orb, flops=5 * 10**9
    )
    pieces = spread(jnp.sum(received[:, :m_aux], axis=0), "orb")
    pieces, half = lax.optimization_barrier((pieces, half))
    third_terms = spread(jnp.sum(pieces, axis=0), "aux").reshape(512, RANK)
    inverse_third = whole(inverse_third_kernel, SQUARE, half, flops=5 * 10**9)
    nu_updated = whole(solve_third_kernel, ROWS, third_terms, inverse_third, scale_both)
    return (a_new / scale_first, b_new / scale_second, nu_updated)


def solution(mesh):
    return jax.shard_map(
        per_device,
        mesh=mesh,
        in_specs=(P(("aux", "orb"), None, None), P(None, ("aux", "orb")), P("orb", None), P()),
        out_specs=(P("aux", None), P("orb", None), P()),
        check_vma=False,
    )
```

```python
import functools

import jax
import jax.numpy as jnp
from jax import lax
from jax.experimental import pallas as pl
from jax.experimental.pallas import tpu as pltpu
from jax.sharding import PartitionSpec as P

P_SIZE = 16384
MU = 4096
NU = 512
RANK = 256
EDGE = 64
SLOTS = 8
WIDE = 16
BLOCK = 32

ridge_weight = 0.5
epsilon = 1e-06
f32 = jnp.float32
bf16 = jnp.bfloat16
params = pltpu.CompilerParams(vmem_limit_bytes=32 * 1024 * 1024)
tile_params = pltpu.CompilerParams(vmem_limit_bytes=48 * 1024 * 1024)


def split(values):
    high = values.astype(bf16)
    return high, (values - high.astype(f32)).astype(bf16)


def weights_of(block):
    high, low = split(block)
    return jnp.concatenate([high, high, low], axis=0)


def split3(values):
    high = values.astype(bf16)
    rest = values - high.astype(f32)
    middle = rest.astype(bf16)
    return high, middle, (rest - middle.astype(f32)).astype(bf16)


def stack_left(values, axis):
    high, middle, low = split3(values)
    return jnp.concatenate([high, high, middle, high, low, middle], axis=axis)


def stack_right(values):
    high, middle, low = split3(values)
    return jnp.concatenate([high, middle, high, low, high, middle], axis=0)


def dot32(left, right):
    return jnp.dot(stack_left(left, 1), stack_right(right), preferred_element_type=f32)


def gram_of(matrix):
    return lax.dot_general(
        stack_left(matrix, 0),
        stack_right(matrix),
        (((0,), (0,)), ((), ())),
        preferred_element_type=f32,
    )


def rows_at(ref, tile_index):
    return ref[pl.ds(pl.multiple_of(tile_index * EDGE, EDGE), EDGE), :]


def tile_kernel(body, kept, list_ref, tile_ref, left_ref, right_ref, out_ref, buffer_ref, arrived):
    def fetch(slot):
        return pltpu.make_async_copy(tile_ref.at[slot], buffer_ref.at[slot], arrived.at[slot])

    for slot in range(SLOTS):

        @pl.when(list_ref[3, slot] > 0)
        def _(slot=slot):
            fetch(slot).start()

    out_ref[:, :kept, :] = jnp.zeros((out_ref.shape[0], kept, RANK), f32)

    @pl.loop(0, SLOTS)
    def _(slot):
        @pl.when(list_ref[3, slot] > 0)
        def _():
            fetch(slot).wait()
            first = lax.rem(list_ref[0, slot], 8)
            second = lax.rem(list_ref[1, slot], 8)
            body(first, second, list_ref[2, slot], buffer_ref.at[slot], left_ref, right_ref, out_ref)


def wide_rows(ref, tile_index, part):
    return ref[pl.ds(pl.multiple_of(tile_index * EDGE + part * WIDE, WIDE), WIDE), :]


def first_body(first, second, third, tile_ref, orb_ref, nu_ref, out_ref):
    weights = weights_of(rows_at(nu_ref, third))
    total = jnp.zeros((EDGE, RANK), f32)
    for part in range(EDGE // WIDE):
        high, low = split(tile_ref[:, part * WIDE * EDGE : (part + 1) * WIDE * EDGE])
        stacked = []
        for j in range(WIDE):
            lanes = slice(j * EDGE, (j + 1) * EDGE)
            stacked.append(jnp.concatenate([high[:, lanes], low[:, lanes], high[:, lanes]], axis=1))
        product = jnp.dot(
            jnp.concatenate(stacked, axis=0), weights, preferred_element_type=f32
        ).reshape(WIDE, EDGE, RANK)
        total = total + jnp.sum(product * wide_rows(orb_ref, second, part)[:, None, :], axis=0)
    out_ref[first, :EDGE, :] = out_ref[first, :EDGE, :] + total


def contract_first(tile_ref, part, weights):
    high, low = split(tile_ref[:, part * WIDE * EDGE : (part + 1) * WIDE * EDGE])
    return lax.dot_general(
        jnp.concatenate([high, low, high], axis=0),
        weights,
        (((0,), (0,)), ((), ())),
        preferred_element_type=f32,
    ).reshape(WIDE, EDGE, RANK)


def second_body(first, second, third, tile_ref, aux_ref, nu_ref, out_ref):
    weights = weights_of(rows_at(aux_ref, first))
    nu_rows = rows_at(nu_ref, third)
    for part in range(EDGE // WIDE):
        addition = jnp.sum(contract_first(tile_ref, part, weights) * nu_rows[None], axis=1)
        at = second * (EDGE // WIDE) + part
        out_ref[at, :WIDE, :] = out_ref[at, :WIDE, :] + addition


def third_body(first, second, third, tile_ref, aux_ref, orb_ref, out_ref):
    weights = weights_of(rows_at(aux_ref, first))
    total = jnp.zeros((EDGE, RANK), f32)
    for part in range(EDGE // WIDE):
        product = contract_first(tile_ref, part, weights)
        total = total + jnp.sum(product * wide_rows(orb_ref, second, part)[:, None, :], axis=0)
    for part in range(EDGE // WIDE):
        at = third * (EDGE // WIDE) + part
        out_ref[at, :WIDE, :] = out_ref[at, :WIDE, :] + total[part * WIDE : (part + 1) * WIDE]


def over_tiles(body, tile_list, tiles, left, right, pieces, room):
    kept = 512 // pieces
    vmem = pl.BlockSpec(memory_space=pltpu.VMEM)
    return pl.pallas_call(
        functools.partial(tile_kernel, body, kept),
        out_shape=jax.ShapeDtypeStruct((pieces, kept + room, RANK), f32),
        grid_spec=pltpu.PrefetchScalarGridSpec(
            num_scalar_prefetch=1,
            grid=(),
            in_specs=[pl.BlockSpec(memory_space=pltpu.HBM), vmem, vmem],
            out_specs=vmem,
            scratch_shapes=[
                pltpu.VMEM((SLOTS, EDGE, EDGE * EDGE), f32),
                pltpu.SemaphoreType.DMA((SLOTS,)),
            ],
        ),
        compiler_params=tile_params,
        cost_estimate=pl.CostEstimate(flops=7 * 10**9, bytes_accessed=10**7, transcendentals=0),
        name=body.__name__.removesuffix("_body") + "_terms",
    )(tile_list, tiles, left, right)


def tree_sum(terms):
    terms = list(terms)
    while len(terms) > 1:
        terms = [sum(terms[i + 1 : i + 2], terms[i]) for i in range(0, len(terms), 2)]
    return terms[0]


def invert_cells(cell):
    def get(i, j):
        return cell[min(i, j), max(i, j)]

    for k in range(0, 8, 2):
        pivots = (k, k + 1)
        others = [i for i in range(8) if i not in pivots]
        top, cross, low = cell[k, k], cell[k, k + 1], cell[k + 1, k + 1]
        factor = 1.0 / (top * low - cross * cross)
        top, cross, low = low * factor, -cross * factor, top * factor
        pair = {
            i: (get(i, k) * top + get(i, k + 1) * cross, get(i, k) * cross + get(i, k + 1) * low)
            for i in others
        }
        fresh = {}
        for i in others:
            for j in others:
                if i <= j:
                    fresh[i, j] = cell[i, j] - pair[i][0] * get(j, k) - pair[i][1] * get(j, k + 1)
            for pivot, value in zip(pivots, pair[i]):
                fresh[min(i, pivot), max(i, pivot)] = value
        fresh[k, k], fresh[k, k + 1], fresh[k + 1, k + 1] = -top, -cross, -low
        cell = fresh
    return cell


def sweep8(matrix, at):
    rows = slice(at, at + 8)
    panel = matrix[rows, :]
    columns = [jnp.broadcast_to(panel[:, at + j : at + j + 1], (8, BLOCK)) for j in range(8)]
    cell = invert_cells(
        {
            (i, j): jnp.broadcast_to(columns[j][i : i + 1, :], (8, BLOCK))
            for i in range(8)
            for j in range(i, 8)
        }
    )
    lane = lax.broadcasted_iota(jnp.int32, (8, BLOCK), 1)
    sub = lax.broadcasted_iota(jnp.int32, (8, BLOCK), 0)
    marked = jnp.where((lane >= at) & (lane < at + 8), jnp.where(lane == sub + at, -1.0, 0.0), panel)
    lines = [jnp.broadcast_to(marked[j : j + 1, :], (8, BLOCK)) for j in range(8)]
    result = [tree_sum(cell[min(i, j), max(i, j)] * lines[j] for j in range(8)) for i in range(8)]
    row_id = lax.broadcasted_iota(jnp.int32, (BLOCK, BLOCK), 0)
    col_id = lax.broadcasted_iota(jnp.int32, (BLOCK, BLOCK), 1)
    in_rows = (row_id >= at) & (row_id < at + 8)
    in_columns = (col_id >= at) & (col_id < at + 8)
    kept = jnp.where(in_rows | in_columns, 0.0, matrix)
    left = jnp.where(in_rows, jnp.where(row_id == col_id, -1.0, 0.0), matrix)
    spreads = [jnp.broadcast_to(left[:, at + j : at + j + 1], (BLOCK, BLOCK)) for j in range(8)]
    parts = []
    for first in range(0, BLOCK, 8):
        group = slice(first, first + 8)
        parts.append(kept[group] + tree_sum(spreads[i][group] * result[i] for i in range(8)))
    return jnp.concatenate(parts, axis=0)


def sweep_blocks(matrix, first, last):
    row_id = lax.broadcasted_iota(jnp.int32, (RANK, RANK), 0)
    col_id = lax.broadcasted_iota(jnp.int32, (RANK, RANK), 1)
    lane = lax.broadcasted_iota(jnp.int32, (BLOCK, RANK), 1)
    sub = lax.broadcasted_iota(jnp.int32, (BLOCK, RANK), 0)
    for at in range(first, last, BLOCK):
        panel = matrix[at : at + BLOCK, :]
        small = panel[:, at : at + BLOCK]
        marked = jnp.where((lane >= at) & (lane < at + BLOCK), jnp.where(lane == sub + at, -1.0, 0.0), panel)
        for step in range(0, BLOCK, 8):
            small = sweep8(small, step)
        result = dot32(small, marked)
        update = lax.dot_general(
            stack_left(marked, 0),
            stack_right(result),
            (((0,), (0,)), ((), ())),
            preferred_element_type=f32,
        )
        in_block = (row_id >= at) & (row_id < at + BLOCK) | (col_id >= at) & (col_id < at + BLOCK)
        matrix = jnp.where(in_block, 0.0, matrix) + update
    return matrix


HALF = RANK // 2
PACKED = jax.ShapeDtypeStruct((HALF + HALF // 2, RANK), f32)
SQUARE = jax.ShapeDtypeStruct((RANK, RANK), f32)
ROWS = jax.ShapeDtypeStruct((512, RANK), f32)
LINE = jax.ShapeDtypeStruct((1, RANK), f32)


def pack(gram):
    corner = gram[HALF:, HALF:]
    corner = jnp.concatenate([corner[: HALF // 2], corner[HALF // 2 :]], axis=1)
    return jnp.concatenate([gram[:HALF], corner], axis=0)


def unpack(packed):
    corner = packed[HALF:]
    corner = jnp.concatenate([corner[:, :HALF], corner[:, HALF:]], axis=0)
    below = jnp.concatenate([packed[:HALF, HALF:].T, corner], axis=1)
    return jnp.concatenate([packed[:HALF], below], axis=0)


def scales(gram, count, axis):
    row_id = lax.broadcasted_iota(jnp.int32, (RANK, RANK), 0)
    col_id = lax.broadcasted_iota(jnp.int32, (RANK, RANK), 1)
    squares = jnp.sum(jnp.where(row_id == col_id, gram, 0.0), axis=axis, keepdims=True)
    return jnp.sqrt(squares * (1.0 / count) + epsilon)


def scaled_gram(gram, count):
    return gram / scales(gram, count, 1) / scales(gram, count, 0) * (1.0 / count)


def system_of(left, right):
    row_id = lax.broadcasted_iota(jnp.int32, (RANK, RANK), 0)
    col_id = lax.broadcasted_iota(jnp.int32, (RANK, RANK), 1)
    return left * right + jnp.where(row_id == col_id, ridge_weight, 0.0)


def inverse_first_kernel(orb_ref, nu_ref, out_ref):
    system = system_of(unpack(orb_ref[...]) * (1.0 / MU), nu_ref[...] * (1.0 / NU))
    out_ref[...] = -sweep_blocks(system, 0, RANK)


def inverse_second_kernel(aux_ref, nu_ref, out_ref, scale_ref):
    scale_ref[...] = scales(aux_ref[...], P_SIZE, 0)
    system = system_of(scaled_gram(aux_ref[...], P_SIZE), nu_ref[...] * (1.0 / NU))
    out_ref[...] = -sweep_blocks(system, 0, RANK)


def half_third_kernel(aux_ref, orb_ref, out_ref, scale_ref, both_ref):
    scale_ref[...] = scales(orb_ref[...], MU, 0)
    both_ref[...] = scales(orb_ref[...], MU, 0) * scales(aux_ref[...], P_SIZE, 0)
    system = system_of(scaled_gram(aux_ref[...], P_SIZE), scaled_gram(orb_ref[...], MU))
    out_ref[...] = sweep_blocks(system, 0, HALF)


def inverse_third_kernel(half_ref, out_ref):
    out_ref[...] = -sweep_blocks(half_ref[...], HALF, RANK)


def packed_gram_kernel(orb_ref, nu_ref, gram_ref, orb_copy_ref, nu_copy_ref):
    gram_ref[...] = pack(gram_of(orb_ref[...]))
    orb_copy_ref[...] = orb_ref[...]
    nu_copy_ref[...] = nu_ref[...]


def gram_kernel(rows_ref, gram_ref):
    gram_ref[...] = gram_of(rows_ref[...])


def solve_first_kernel(terms_ref, inverse_ref, out_ref, gram_ref):
    out_ref[...] = dot32(terms_ref[...], inverse_ref[...])
    gram_ref[...] = gram_of(out_ref[...])


def solve_second_kernel(terms_ref, inverse_ref, scale_ref, out_ref, gram_ref):
    out_ref[...] = dot32(terms_ref[...] / scale_ref[...], inverse_ref[...])
    gram_ref[...] = gram_of(out_ref[...])


def solve_third_kernel(terms_ref, inverse_ref, scale_ref, out_ref):
    values = dot32(terms_ref[...] / scale_ref[...], inverse_ref[...])
    squares = jnp.sum(values * values, axis=0, keepdims=True)
    out_ref[...] = values / jnp.sqrt(squares * (1.0 / NU) + epsilon)


def whole(kernel, out_shape, *operands, flops=10**9):
    return pl.pallas_call(
        kernel,
        out_shape=out_shape,
        compiler_params=params,
        cost_estimate=pl.CostEstimate(flops=flops, bytes_accessed=10**6, transcendentals=0),
        name=kernel.__name__.removesuffix("_kernel"),
    )(*operands)


def exchange(pieces, axis):
    return lax.all_to_all(pieces, axis, 0, 0)


def spread(piece, axis):
    count = lax.axis_size(axis)
    return exchange(jnp.broadcast_to(piece[None], (count,) + piece.shape), axis)


def beside(pieces, slab):
    filling = jnp.broadcast_to(slab[None], pieces.shape[:1] + slab.shape)
    return lax.dynamic_update_slice(pieces, filling, (0, pieces.shape[1] - slab.shape[0], 0))


def per_device(tiles, tile_list, orb_factor, nu_factor):
    n_aux = lax.axis_size("aux")
    n_orb = lax.axis_size("orb")
    m_orb = 512 // n_orb
    m_aux = 512 // n_aux
    g_aux = RANK // n_aux
    g_orb = PACKED.shape[0] // n_orb

    gram_orb, orb_factor, nu_factor = whole(
        packed_gram_kernel, (PACKED, ROWS, ROWS), orb_factor, nu_factor
    )
    slab_orb = jnp.sum(exchange(gram_orb.reshape(n_orb, g_orb, RANK), "orb"), axis=0)
    partial_first = over_tiles(first_body, tile_list, tiles, orb_factor, nu_factor, n_orb, g_orb)
    received = exchange(beside(partial_first, slab_orb), "orb")
    nu_later, _ = lax.optimization_barrier((nu_factor, partial_first))
    gram_nu = whole(gram_kernel, SQUARE, nu_later)
    gram_orb = received[:, m_orb:].reshape(PACKED.shape)
    first_terms = spread(jnp.sum(received[:, :m_orb], axis=0), "orb").reshape(512, RANK)
    inverse_first = whole(inverse_first_kernel, SQUARE, gram_orb, gram_nu, flops=10**10)

    a_new, gram_part = whole(solve_first_kernel, (ROWS, SQUARE), first_terms, inverse_first)
    slab_aux = jnp.sum(exchange(gram_part.reshape(n_aux, g_aux, RANK), "aux"), axis=0)
    partial_second = over_tiles(second_body, tile_list, tiles, a_new, nu_factor, n_aux, g_aux)
    received = exchange(beside(partial_second, slab_aux), "aux")
    gram_aux = received[:, m_aux:].reshape(RANK, RANK)
    second_terms = spread(jnp.sum(received[:, :m_aux], axis=0), "aux").reshape(512, RANK)
    inverse_second, scale_first = whole(
        inverse_second_kernel, (SQUARE, LINE), gram_aux, gram_nu, flops=10**10
    )

    b_new, gram_part = whole(
        solve_second_kernel, (ROWS, SQUARE), second_terms, inverse_second, scale_first
    )
    slab = lax.dynamic_slice_in_dim(gram_part, lax.axis_index("aux") * g_aux, g_aux, 0)
    slab_orb = jnp.sum(spread(slab, "orb"), axis=0)
    partial_third = over_tiles(third_body, tile_list, tiles, a_new, b_new, n_aux, g_aux)
    received = exchange(beside(partial_third, slab_orb), "aux")
    gram_orb = received[:, m_aux:].reshape(RANK, RANK)
    half, scale_second, scale_both = whole(
        half_third_kernel, (SQUARE, LINE, LINE), gram_aux, gram_orb, flops=5 * 10**9
    )
    pieces = spread(jnp.sum(received[:, :m_aux], axis=0), "orb")
    pieces, half = lax.optimization_barrier((pieces, half))
    third_terms = spread(jnp.sum(pieces, axis=0), "aux").reshape(512, RANK)
    inverse_third = whole(inverse_third_kernel, SQUARE, half, flops=5 * 10**9)
    nu_updated = whole(solve_third_kernel, ROWS, third_terms, inverse_third, scale_both)
    return (a_new / scale_first, b_new / scale_second, nu_updated)


def solution(mesh):
    return jax.shard_map(
        per_device,
        mesh=mesh,
        in_specs=(P(("aux", "orb"), None, None), P(None, ("aux", "orb")), P("orb", None), P()),
        out_specs=(P("aux", None), P("orb", None), P()),
        check_vma=False,
    )
```

```python
import functools

import jax
import jax.numpy as jnp
from jax import lax
from jax.experimental import pallas as pl
from jax.experimental.pallas import tpu as pltpu
from jax.sharding import PartitionSpec as P

P_SIZE = 16384
MU = 4096
NU = 512
RANK = 256
EDGE = 64
SLOTS = 8
WIDE = 16
BLOCK = 32

ridge_weight = 0.5
epsilon = 1e-06
f32 = jnp.float32
bf16 = jnp.bfloat16
params = pltpu.CompilerParams(vmem_limit_bytes=32 * 1024 * 1024)
tile_params = pltpu.CompilerParams(vmem_limit_bytes=48 * 1024 * 1024)


def split(values):
    high = values.astype(bf16)
    return high, (values - high.astype(f32)).astype(bf16)


def weights_of(block):
    high, low = split(block)
    return jnp.concatenate([high, high, low], axis=0)


def split3(values):
    high = values.astype(bf16)
    rest = values - high.astype(f32)
    middle = rest.astype(bf16)
    return high, middle, (rest - middle.astype(f32)).astype(bf16)


def stack_left(values, axis):
    high, middle, low = split3(values)
    return jnp.concatenate([high, high, middle, high, low, middle], axis=axis)


def stack_right(values):
    high, middle, low = split3(values)
    return jnp.concatenate([high, middle, high, low, high, middle], axis=0)


def dot32(left, right):
    return jnp.dot(stack_left(left, 1), stack_right(right), preferred_element_type=f32)


def gram_of(matrix):
    return lax.dot_general(
        stack_left(matrix, 0),
        stack_right(matrix),
        (((0,), (0,)), ((), ())),
        preferred_element_type=f32,
    )


def rows_at(ref, tile_index):
    return ref[pl.ds(pl.multiple_of(tile_index * EDGE, EDGE), EDGE), :]


def tile_kernel(body, kept, list_ref, tile_ref, left_ref, right_ref, out_ref, buffer_ref, arrived):
    def fetch(slot):
        return pltpu.make_async_copy(tile_ref.at[slot], buffer_ref.at[slot], arrived.at[slot])

    for slot in range(SLOTS):

        @pl.when(list_ref[3, slot] > 0)
        def _(slot=slot):
            fetch(slot).start()

    out_ref[:, :kept, :] = jnp.zeros((out_ref.shape[0], kept, RANK), f32)

    @pl.loop(0, SLOTS)
    def _(slot):
        @pl.when(list_ref[3, slot] > 0)
        def _():
            fetch(slot).wait()
            first = lax.rem(list_ref[0, slot], 8)
            second = lax.rem(list_ref[1, slot], 8)
            body(first, second, list_ref[2, slot], buffer_ref.at[slot], left_ref, right_ref, out_ref)


def wide_rows(ref, tile_index, part):
    return ref[pl.ds(pl.multiple_of(tile_index * EDGE + part * WIDE, WIDE), WIDE), :]


def first_body(first, second, third, tile_ref, orb_ref, nu_ref, out_ref):
    weights = weights_of(rows_at(nu_ref, third))
    total = jnp.zeros((EDGE, RANK), f32)
    for part in range(EDGE // WIDE):
        high, low = split(tile_ref[:, part * WIDE * EDGE : (part + 1) * WIDE * EDGE])
        stacked = []
        for j in range(WIDE):
            lanes = slice(j * EDGE, (j + 1) * EDGE)
            stacked.append(jnp.concatenate([high[:, lanes], low[:, lanes], high[:, lanes]], axis=1))
        product = jnp.dot(
            jnp.concatenate(stacked, axis=0), weights, preferred_element_type=f32
        ).reshape(WIDE, EDGE, RANK)
        total = total + jnp.sum(product * wide_rows(orb_ref, second, part)[:, None, :], axis=0)
    out_ref[first, :EDGE, :] = out_ref[first, :EDGE, :] + total


def contract_first(tile_ref, part, weights):
    high, low = split(tile_ref[:, part * WIDE * EDGE : (part + 1) * WIDE * EDGE])
    return lax.dot_general(
        jnp.concatenate([high, low, high], axis=0),
        weights,
        (((0,), (0,)), ((), ())),
        preferred_element_type=f32,
    ).reshape(WIDE, EDGE, RANK)


def second_body(first, second, third, tile_ref, aux_ref, nu_ref, out_ref):
    weights = weights_of(rows_at(aux_ref, first))
    nu_rows = rows_at(nu_ref, third)
    for part in range(EDGE // WIDE):
        addition = jnp.sum(contract_first(tile_ref, part, weights) * nu_rows[None], axis=1)
        at = second * (EDGE // WIDE) + part
        out_ref[at, :WIDE, :] = out_ref[at, :WIDE, :] + addition


def third_body(first, second, third, tile_ref, aux_ref, orb_ref, out_ref):
    weights = weights_of(rows_at(aux_ref, first))
    total = jnp.zeros((EDGE, RANK), f32)
    for part in range(EDGE // WIDE):
        product = contract_first(tile_ref, part, weights)
        total = total + jnp.sum(product * wide_rows(orb_ref, second, part)[:, None, :], axis=0)
    for part in range(EDGE // WIDE):
        at = third * (EDGE // WIDE) + part
        out_ref[at, :WIDE, :] = out_ref[at, :WIDE, :] + total[part * WIDE : (part + 1) * WIDE]


def over_tiles(body, tile_list, tiles, left, right, pieces, room):
    kept = 512 // pieces
    vmem = pl.BlockSpec(memory_space=pltpu.VMEM)
    return pl.pallas_call(
        functools.partial(tile_kernel, body, kept),
        out_shape=jax.ShapeDtypeStruct((pieces, kept + room, RANK), f32),
        grid_spec=pltpu.PrefetchScalarGridSpec(
            num_scalar_prefetch=1,
            grid=(),
            in_specs=[pl.BlockSpec(memory_space=pltpu.HBM), vmem, vmem],
            out_specs=vmem,
            scratch_shapes=[
                pltpu.VMEM((SLOTS, EDGE, EDGE * EDGE), f32),
                pltpu.SemaphoreType.DMA((SLOTS,)),
            ],
        ),
        compiler_params=tile_params,
        cost_estimate=pl.CostEstimate(flops=7 * 10**9, bytes_accessed=10**7, transcendentals=0),
        name=body.__name__.removesuffix("_body") + "_terms",
    )(tile_list, tiles, left, right)


def tree_sum(terms):
    terms = list(terms)
    while len(terms) > 1:
        terms = [sum(terms[i + 1 : i + 2], terms[i]) for i in range(0, len(terms), 2)]
    return terms[0]


def invert_cells(cell):
    def get(i, j):
        return cell[min(i, j), max(i, j)]

    for k in range(0, 8, 2):
        pivots = (k, k + 1)
        others = [i for i in range(8) if i not in pivots]
        top, cross, low = cell[k, k], cell[k, k + 1], cell[k + 1, k + 1]
        factor = 1.0 / (top * low - cross * cross)
        top, cross, low = low * factor, -cross * factor, top * factor
        pair = {
            i: (get(i, k) * top + get(i, k + 1) * cross, get(i, k) * cross + get(i, k + 1) * low)
            for i in others
        }
        fresh = {}
        for i in others:
            for j in others:
                if i <= j:
                    fresh[i, j] = cell[i, j] - pair[i][0] * get(j, k) - pair[i][1] * get(j, k + 1)
            for pivot, value in zip(pivots, pair[i]):
                fresh[min(i, pivot), max(i, pivot)] = value
        fresh[k, k], fresh[k, k + 1], fresh[k + 1, k + 1] = -top, -cross, -low
        cell = fresh
    return cell


def sweep8(matrix, at):
    rows = slice(at, at + 8)
    panel = matrix[rows, :]
    columns = [jnp.broadcast_to(panel[:, at + j : at + j + 1], (8, BLOCK)) for j in range(8)]
    cell = invert_cells(
        {
            (i, j): jnp.broadcast_to(columns[j][i : i + 1, :], (8, BLOCK))
            for i in range(8)
            for j in range(i, 8)
        }
    )
    lane = lax.broadcasted_iota(jnp.int32, (8, BLOCK), 1)
    sub = lax.broadcasted_iota(jnp.int32, (8, BLOCK), 0)
    marked = jnp.where((lane >= at) & (lane < at + 8), jnp.where(lane == sub + at, -1.0, 0.0), panel)
    lines = [jnp.broadcast_to(marked[j : j + 1, :], (8, BLOCK)) for j in range(8)]
    result = [tree_sum(cell[min(i, j), max(i, j)] * lines[j] for j in range(8)) for i in range(8)]
    row_id = lax.broadcasted_iota(jnp.int32, (BLOCK, BLOCK), 0)
    col_id = lax.broadcasted_iota(jnp.int32, (BLOCK, BLOCK), 1)
    in_rows = (row_id >= at) & (row_id < at + 8)
    in_columns = (col_id >= at) & (col_id < at + 8)
    kept = jnp.where(in_rows | in_columns, 0.0, matrix)
    left = jnp.where(in_rows, jnp.where(row_id == col_id, -1.0, 0.0), matrix)
    spreads = [jnp.broadcast_to(left[:, at + j : at + j + 1], (BLOCK, BLOCK)) for j in range(8)]
    parts = []
    for first in range(0, BLOCK, 8):
        group = slice(first, first + 8)
        parts.append(kept[group] + tree_sum(spreads[i][group] * result[i] for i in range(8)))
    return jnp.concatenate(parts, axis=0)


def sweep_blocks(matrix, first, last):
    row_id = lax.broadcasted_iota(jnp.int32, (RANK, RANK), 0)
    col_id = lax.broadcasted_iota(jnp.int32, (RANK, RANK), 1)
    lane = lax.broadcasted_iota(jnp.int32, (BLOCK, RANK), 1)
    sub = lax.broadcasted_iota(jnp.int32, (BLOCK, RANK), 0)
    for at in range(first, last, BLOCK):
        panel = matrix[at : at + BLOCK, :]
        small = panel[:, at : at + BLOCK]
        marked = jnp.where((lane >= at) & (lane < at + BLOCK), jnp.where(lane == sub + at, -1.0, 0.0), panel)
        for step in range(0, BLOCK, 8):
            small = sweep8(small, step)
        result = dot32(small, marked)
        update = lax.dot_general(
            stack_left(marked, 0),
            stack_right(result),
            (((0,), (0,)), ((), ())),
            preferred_element_type=f32,
        )
        in_block = (row_id >= at) & (row_id < at + BLOCK) | (col_id >= at) & (col_id < at + BLOCK)
        matrix = jnp.where(in_block, 0.0, matrix) + update
    return matrix


HALF = RANK // 2
FIRST_PART = 96
PACKED = jax.ShapeDtypeStruct((HALF + HALF // 2, RANK), f32)
SQUARE = jax.ShapeDtypeStruct((RANK, RANK), f32)
ROWS = jax.ShapeDtypeStruct((512, RANK), f32)
LINE = jax.ShapeDtypeStruct((1, RANK), f32)


def pack(gram):
    corner = gram[HALF:, HALF:]
    corner = jnp.concatenate([corner[: HALF // 2], corner[HALF // 2 :]], axis=1)
    return jnp.concatenate([gram[:HALF], corner], axis=0)


def unpack(packed):
    corner = packed[HALF:]
    corner = jnp.concatenate([corner[:, :HALF], corner[:, HALF:]], axis=0)
    below = jnp.concatenate([packed[:HALF, HALF:].T, corner], axis=1)
    return jnp.concatenate([packed[:HALF], below], axis=0)


def scales(gram, count, axis):
    row_id = lax.broadcasted_iota(jnp.int32, (RANK, RANK), 0)
    col_id = lax.broadcasted_iota(jnp.int32, (RANK, RANK), 1)
    squares = jnp.sum(jnp.where(row_id == col_id, gram, 0.0), axis=axis, keepdims=True)
    return jnp.sqrt(squares * (1.0 / count) + epsilon)


def scaled_gram(gram, count):
    return gram / scales(gram, count, 1) / scales(gram, count, 0) * (1.0 / count)


def system_of(left, right):
    row_id = lax.broadcasted_iota(jnp.int32, (RANK, RANK), 0)
    col_id = lax.broadcasted_iota(jnp.int32, (RANK, RANK), 1)
    return left * right + jnp.where(row_id == col_id, ridge_weight, 0.0)


def inverse_first_kernel(orb_ref, nu_ref, out_ref):
    system = system_of(unpack(orb_ref[...]) * (1.0 / MU), nu_ref[...] * (1.0 / NU))
    out_ref[...] = -sweep_blocks(system, 0, RANK)


def inverse_second_kernel(aux_ref, nu_ref, out_ref, scale_ref):
    scale_ref[...] = scales(aux_ref[...], P_SIZE, 0)
    system = system_of(scaled_gram(aux_ref[...], P_SIZE), nu_ref[...] * (1.0 / NU))
    out_ref[...] = -sweep_blocks(system, 0, RANK)


def begin_third_kernel(aux_ref, orb_ref, out_ref, scale_ref, both_ref):
    scale_ref[...] = scales(orb_ref[...], MU, 0)
    both_ref[...] = scales(orb_ref[...], MU, 0) * scales(aux_ref[...], P_SIZE, 0)
    system = system_of(scaled_gram(aux_ref[...], P_SIZE), scaled_gram(orb_ref[...], MU))
    out_ref[...] = sweep_blocks(system, 0, FIRST_PART)


def inverse_third_kernel(part_ref, out_ref):
    out_ref[...] = -sweep_blocks(part_ref[...], FIRST_PART, RANK)


def packed_gram_kernel(rows_ref, gram_ref, copy_ref):
    gram_ref[...] = pack(gram_of(rows_ref[...]))
    copy_ref[...] = rows_ref[...]


def gram_kernel(rows_ref, gram_ref):
    gram_ref[...] = gram_of(rows_ref[...])


def solve_first_kernel(terms_ref, inverse_ref, out_ref, gram_ref):
    out_ref[...] = dot32(terms_ref[...], inverse_ref[...])
    gram_ref[...] = gram_of(out_ref[...])


def solve_second_kernel(terms_ref, inverse_ref, scale_ref, out_ref, gram_ref):
    out_ref[...] = dot32(terms_ref[...] / scale_ref[...], inverse_ref[...])
    gram_ref[...] = gram_of(out_ref[...])


def solve_third_kernel(terms_ref, inverse_ref, scale_ref, out_ref):
    values = dot32(terms_ref[...] / scale_ref[...], inverse_ref[...])
    squares = jnp.sum(values * values, axis=0, keepdims=True)
    out_ref[...] = values / jnp.sqrt(squares * (1.0 / NU) + epsilon)


def whole(kernel, out_shape, *operands, flops=10**9):
    return pl.pallas_call(
        kernel,
        out_shape=out_shape,
        compiler_params=params,
        cost_estimate=pl.CostEstimate(flops=flops, bytes_accessed=10**6, transcendentals=0),
        name=kernel.__name__.removesuffix("_kernel"),
    )(*operands)


def in_hbm(operand):
    return pltpu.with_memory_space_constraint(operand, pltpu.HBM)


def exchange(pieces, axis):
    return lax.all_to_all(pieces, axis, 0, 0)


def spread(piece, axis):
    count = lax.axis_size(axis)
    return exchange(jnp.broadcast_to(piece[None], (count,) + piece.shape), axis)


def beside(pieces, slab):
    filling = jnp.broadcast_to(slab[None], pieces.shape[:1] + slab.shape)
    return lax.dynamic_update_slice(pieces, filling, (0, pieces.shape[1] - slab.shape[0], 0))


def per_device(tiles, tile_list, orb_factor, nu_factor):
    n_aux = lax.axis_size("aux")
    n_orb = lax.axis_size("orb")
    m_orb = 512 // n_orb
    m_aux = 512 // n_aux
    g_aux = RANK // n_aux
    g_orb = PACKED.shape[0] // n_orb

    tile_list = in_hbm(tile_list)
    gram_orb, orb_factor = whole(packed_gram_kernel, (PACKED, ROWS), in_hbm(orb_factor))
    slab_orb = jnp.sum(exchange(gram_orb.reshape(n_orb, g_orb, RANK), "orb"), axis=0)
    partial_first = over_tiles(
        first_body, tile_list, tiles, orb_factor, in_hbm(nu_factor), n_orb, g_orb
    )
    nu_later, slab_orb = lax.optimization_barrier((nu_factor, slab_orb))
    received = exchange(beside(partial_first, slab_orb), "orb")
    gram_nu = whole(gram_kernel, SQUARE, nu_later)
    gram_orb = received[:, m_orb:].reshape(PACKED.shape)
    first_terms = spread(jnp.sum(received[:, :m_orb], axis=0), "orb").reshape(512, RANK)
    inverse_first = whole(inverse_first_kernel, SQUARE, gram_orb, gram_nu, flops=10**10)

    a_new, gram_part = whole(solve_first_kernel, (ROWS, SQUARE), first_terms, inverse_first)
    slab_aux = jnp.sum(exchange(gram_part.reshape(n_aux, g_aux, RANK), "aux"), axis=0)
    partial_second = over_tiles(second_body, tile_list, tiles, a_new, nu_factor, n_aux, g_aux)
    received = exchange(beside(partial_second, slab_aux), "aux")
    gram_aux = received[:, m_aux:].reshape(RANK, RANK)
    second_terms = spread(jnp.sum(received[:, :m_aux], axis=0), "aux").reshape(512, RANK)
    inverse_second, scale_first = whole(
        inverse_second_kernel, (SQUARE, LINE), gram_aux, gram_nu, flops=10**10
    )

    b_new, gram_part = whole(
        solve_second_kernel, (ROWS, SQUARE), second_terms, inverse_second, scale_first
    )
    slab = lax.dynamic_slice_in_dim(gram_part, lax.axis_index("aux") * g_aux, g_aux, 0)
    slab_orb = jnp.sum(spread(slab, "orb"), axis=0)
    partial_third = over_tiles(third_body, tile_list, tiles, a_new, b_new, n_aux, g_aux)
    received = exchange(beside(partial_third, slab_orb), "aux")
    gram_orb = received[:, m_aux:].reshape(RANK, RANK)
    begun, scale_second, scale_both = whole(
        begin_third_kernel, (SQUARE, LINE, LINE), gram_aux, gram_orb, flops=5 * 10**9
    )
    pieces = spread(jnp.sum(received[:, :m_aux], axis=0), "orb")
    pieces, begun = lax.optimization_barrier((pieces, begun))
    third_terms = spread(jnp.sum(pieces, axis=0), "aux").reshape(512, RANK)
    inverse_third = whole(inverse_third_kernel, SQUARE, begun, flops=5 * 10**9)
    nu_updated = whole(solve_third_kernel, ROWS, third_terms, inverse_third, scale_both)
    return (a_new / scale_first, b_new / scale_second, nu_updated)


def solution(mesh):
    return jax.shard_map(
        per_device,
        mesh=mesh,
        in_specs=(P(("aux", "orb"), None, None), P(None, ("aux", "orb")), P("orb", None), P()),
        out_specs=(P("aux", None), P("orb", None), P()),
        check_vma=False,
    )
```

```python
import functools

import jax
import jax.numpy as jnp
from jax import lax
from jax.experimental import pallas as pl
from jax.experimental.pallas import tpu as pltpu
from jax.sharding import PartitionSpec as P

P_SIZE = 16384
MU = 4096
NU = 512
RANK = 256
EDGE = 64
SLOTS = 8
WIDE = 16
BLOCK = 32

ridge_weight = 0.5
epsilon = 1e-06
f32 = jnp.float32
bf16 = jnp.bfloat16
params = pltpu.CompilerParams(vmem_limit_bytes=32 * 1024 * 1024)
tile_params = pltpu.CompilerParams(vmem_limit_bytes=48 * 1024 * 1024)


def split(values):
    high = values.astype(bf16)
    return high, (values - high.astype(f32)).astype(bf16)


def weights_of(block):
    high, low = split(block)
    return jnp.concatenate([high, high, low], axis=0)


def split3(values):
    high = values.astype(bf16)
    rest = values - high.astype(f32)
    middle = rest.astype(bf16)
    return high, middle, (rest - middle.astype(f32)).astype(bf16)


def stack_left(values, axis):
    high, middle, low = split3(values)
    return jnp.concatenate([high, high, middle, high, low, middle], axis=axis)


def stack_right(values):
    high, middle, low = split3(values)
    return jnp.concatenate([high, middle, high, low, high, middle], axis=0)


def dot32(left, right):
    return jnp.dot(stack_left(left, 1), stack_right(right), preferred_element_type=f32)


def gram_of(matrix):
    return lax.dot_general(
        stack_left(matrix, 0),
        stack_right(matrix),
        (((0,), (0,)), ((), ())),
        preferred_element_type=f32,
    )


def rows_at(ref, tile_index):
    return ref[pl.ds(pl.multiple_of(tile_index * EDGE, EDGE), EDGE), :]


def tile_kernel(body, kept, list_ref, tile_ref, left_ref, right_ref, out_ref, buffer_ref, arrived):
    def fetch(slot):
        return pltpu.make_async_copy(tile_ref.at[slot], buffer_ref.at[slot], arrived.at[slot])

    for slot in range(SLOTS):

        @pl.when(list_ref[3, slot] > 0)
        def _(slot=slot):
            fetch(slot).start()

    out_ref[:, :kept, :] = jnp.zeros((out_ref.shape[0], kept, RANK), f32)

    @pl.loop(0, SLOTS)
    def _(slot):
        @pl.when(list_ref[3, slot] > 0)
        def _():
            fetch(slot).wait()
            first = lax.rem(list_ref[0, slot], 8)
            second = lax.rem(list_ref[1, slot], 8)
            body(first, second, list_ref[2, slot], buffer_ref.at[slot], left_ref, right_ref, out_ref)


def wide_rows(ref, tile_index, part):
    return ref[pl.ds(pl.multiple_of(tile_index * EDGE + part * WIDE, WIDE), WIDE), :]


def first_body(first, second, third, tile_ref, orb_ref, nu_ref, out_ref):
    weights = weights_of(rows_at(nu_ref, third))
    total = jnp.zeros((EDGE, RANK), f32)
    for part in range(EDGE // WIDE):
        high, low = split(tile_ref[:, part * WIDE * EDGE : (part + 1) * WIDE * EDGE])
        stacked = []
        for j in range(WIDE):
            lanes = slice(j * EDGE, (j + 1) * EDGE)
            stacked.append(jnp.concatenate([high[:, lanes], low[:, lanes], high[:, lanes]], axis=1))
        product = jnp.dot(
            jnp.concatenate(stacked, axis=0), weights, preferred_element_type=f32
        ).reshape(WIDE, EDGE, RANK)
        total = total + jnp.sum(product * wide_rows(orb_ref, second, part)[:, None, :], axis=0)
    out_ref[first, :EDGE, :] = out_ref[first, :EDGE, :] + total


def contract_first(tile_ref, part, weights):
    high, low = split(tile_ref[:, part * WIDE * EDGE : (part + 1) * WIDE * EDGE])
    return lax.dot_general(
        jnp.concatenate([high, low, high], axis=0),
        weights,
        (((0,), (0,)), ((), ())),
        preferred_element_type=f32,
    ).reshape(WIDE, EDGE, RANK)


def second_body(first, second, third, tile_ref, aux_ref, nu_ref, out_ref):
    weights = weights_of(rows_at(aux_ref, first))
    nu_rows = rows_at(nu_ref, third)
    for part in range(EDGE // WIDE):
        addition = jnp.sum(contract_first(tile_ref, part, weights) * nu_rows[None], axis=1)
        at = second * (EDGE // WIDE) + part
        out_ref[at, :WIDE, :] = out_ref[at, :WIDE, :] + addition


def third_body(first, second, third, tile_ref, aux_ref, orb_ref, out_ref):
    weights = weights_of(rows_at(aux_ref, first))
    total = jnp.zeros((EDGE, RANK), f32)
    for part in range(EDGE // WIDE):
        product = contract_first(tile_ref, part, weights)
        total = total + jnp.sum(product * wide_rows(orb_ref, second, part)[:, None, :], axis=0)
    for part in range(EDGE // WIDE):
        at = third * (EDGE // WIDE) + part
        out_ref[at, :WIDE, :] = out_ref[at, :WIDE, :] + total[part * WIDE : (part + 1) * WIDE]


def over_tiles(body, tile_list, tiles, left, right, pieces, room):
    kept = 512 // pieces
    vmem = pl.BlockSpec(memory_space=pltpu.VMEM)
    return pl.pallas_call(
        functools.partial(tile_kernel, body, kept),
        out_shape=jax.ShapeDtypeStruct((pieces, kept + room, RANK), f32),
        grid_spec=pltpu.PrefetchScalarGridSpec(
            num_scalar_prefetch=1,
            grid=(),
            in_specs=[pl.BlockSpec(memory_space=pltpu.HBM), vmem, vmem],
            out_specs=vmem,
            scratch_shapes=[
                pltpu.VMEM((SLOTS, EDGE, EDGE * EDGE), f32),
                pltpu.SemaphoreType.DMA((SLOTS,)),
            ],
        ),
        compiler_params=tile_params,
        cost_estimate=pl.CostEstimate(flops=7 * 10**9, bytes_accessed=10**7, transcendentals=0),
        name=body.__name__.removesuffix("_body") + "_terms",
    )(tile_list, tiles, left, right)


def tree_sum(terms):
    terms = list(terms)
    while len(terms) > 1:
        terms = [sum(terms[i + 1 : i + 2], terms[i]) for i in range(0, len(terms), 2)]
    return terms[0]


def invert_cells(cell):
    def get(i, j):
        return cell[min(i, j), max(i, j)]

    for k in range(0, 8, 2):
        pivots = (k, k + 1)
        others = [i for i in range(8) if i not in pivots]
        top, cross, low = cell[k, k], cell[k, k + 1], cell[k + 1, k + 1]
        factor = 1.0 / (top * low - cross * cross)
        top, cross, low = low * factor, -cross * factor, top * factor
        pair = {
            i: (get(i, k) * top + get(i, k + 1) * cross, get(i, k) * cross + get(i, k + 1) * low)
            for i in others
        }
        fresh = {}
        for i in others:
            for j in others:
                if i <= j:
                    fresh[i, j] = cell[i, j] - pair[i][0] * get(j, k) - pair[i][1] * get(j, k + 1)
            for pivot, value in zip(pivots, pair[i]):
                fresh[min(i, pivot), max(i, pivot)] = value
        fresh[k, k], fresh[k, k + 1], fresh[k + 1, k + 1] = -top, -cross, -low
        cell = fresh
    return cell


def sweep8(matrix, at):
    rows = slice(at, at + 8)
    panel = matrix[rows, :]
    columns = [jnp.broadcast_to(panel[:, at + j : at + j + 1], (8, BLOCK)) for j in range(8)]
    cell = invert_cells(
        {
            (i, j): jnp.broadcast_to(columns[j][i : i + 1, :], (8, BLOCK))
            for i in range(8)
            for j in range(i, 8)
        }
    )
    lane = lax.broadcasted_iota(jnp.int32, (8, BLOCK), 1)
    sub = lax.broadcasted_iota(jnp.int32, (8, BLOCK), 0)
    marked = jnp.where((lane >= at) & (lane < at + 8), jnp.where(lane == sub + at, -1.0, 0.0), panel)
    lines = [jnp.broadcast_to(marked[j : j + 1, :], (8, BLOCK)) for j in range(8)]
    result = [tree_sum(cell[min(i, j), max(i, j)] * lines[j] for j in range(8)) for i in range(8)]
    row_id = lax.broadcasted_iota(jnp.int32, (BLOCK, BLOCK), 0)
    col_id = lax.broadcasted_iota(jnp.int32, (BLOCK, BLOCK), 1)
    in_rows = (row_id >= at) & (row_id < at + 8)
    in_columns = (col_id >= at) & (col_id < at + 8)
    kept = jnp.where(in_rows | in_columns, 0.0, matrix)
    left = jnp.where(in_rows, jnp.where(row_id == col_id, -1.0, 0.0), matrix)
    spreads = [jnp.broadcast_to(left[:, at + j : at + j + 1], (BLOCK, BLOCK)) for j in range(8)]
    parts = []
    for first in range(0, BLOCK, 8):
        group = slice(first, first + 8)
        parts.append(kept[group] + tree_sum(spreads[i][group] * result[i] for i in range(8)))
    return jnp.concatenate(parts, axis=0)


def sweep_blocks(matrix, first, last):
    row_id = lax.broadcasted_iota(jnp.int32, (RANK, RANK), 0)
    col_id = lax.broadcasted_iota(jnp.int32, (RANK, RANK), 1)
    lane = lax.broadcasted_iota(jnp.int32, (BLOCK, RANK), 1)
    sub = lax.broadcasted_iota(jnp.int32, (BLOCK, RANK), 0)
    for at in range(first, last, BLOCK):
        panel = matrix[at : at + BLOCK, :]
        small = panel[:, at : at + BLOCK]
        marked = jnp.where((lane >= at) & (lane < at + BLOCK), jnp.where(lane == sub + at, -1.0, 0.0), panel)
        for step in range(0, BLOCK, 8):
            small = sweep8(small, step)
        result = dot32(small, marked)
        update = lax.dot_general(
            stack_left(marked, 0),
            stack_right(result),
            (((0,), (0,)), ((), ())),
            preferred_element_type=f32,
        )
        in_block = (row_id >= at) & (row_id < at + BLOCK) | (col_id >= at) & (col_id < at + BLOCK)
        matrix = jnp.where(in_block, 0.0, matrix) + update
    return matrix


HALF = RANK // 2
FIRST_PART = 128
PACKED = jax.ShapeDtypeStruct((HALF + HALF // 2, RANK), f32)
SQUARE = jax.ShapeDtypeStruct((RANK, RANK), f32)
ROWS = jax.ShapeDtypeStruct((512, RANK), f32)
LINE = jax.ShapeDtypeStruct((1, RANK), f32)


def pack(gram):
    corner = gram[HALF:, HALF:]
    corner = jnp.concatenate([corner[: HALF // 2], corner[HALF // 2 :]], axis=1)
    return jnp.concatenate([gram[:HALF], corner], axis=0)


def unpack(packed):
    corner = packed[HALF:]
    corner = jnp.concatenate([corner[:, :HALF], corner[:, HALF:]], axis=0)
    below = jnp.concatenate([packed[:HALF, HALF:].T, corner], axis=1)
    return jnp.concatenate([packed[:HALF], below], axis=0)


def scales(gram, count, axis):
    row_id = lax.broadcasted_iota(jnp.int32, (RANK, RANK), 0)
    col_id = lax.broadcasted_iota(jnp.int32, (RANK, RANK), 1)
    squares = jnp.sum(jnp.where(row_id == col_id, gram, 0.0), axis=axis, keepdims=True)
    return jnp.sqrt(squares * (1.0 / count) + epsilon)


def scaled_gram(gram, count):
    return gram / scales(gram, count, 1) / scales(gram, count, 0) * (1.0 / count)


def system_of(left, right):
    row_id = lax.broadcasted_iota(jnp.int32, (RANK, RANK), 0)
    col_id = lax.broadcasted_iota(jnp.int32, (RANK, RANK), 1)
    return left * right + jnp.where(row_id == col_id, ridge_weight, 0.0)


def inverse_first_kernel(orb_ref, nu_ref, out_ref):
    system = system_of(unpack(orb_ref[...]) * (1.0 / MU), nu_ref[...] * (1.0 / NU))
    out_ref[...] = -sweep_blocks(system, 0, RANK)


def inverse_second_kernel(aux_ref, nu_ref, out_ref, scale_ref):
    scale_ref[...] = scales(aux_ref[...], P_SIZE, 0)
    system = system_of(scaled_gram(aux_ref[...], P_SIZE), nu_ref[...] * (1.0 / NU))
    out_ref[...] = -sweep_blocks(system, 0, RANK)


def begin_third_kernel(aux_ref, orb_ref, out_ref, scale_ref, both_ref):
    scale_ref[...] = scales(orb_ref[...], MU, 0)
    both_ref[...] = scales(orb_ref[...], MU, 0) * scales(aux_ref[...], P_SIZE, 0)
    system = system_of(scaled_gram(aux_ref[...], P_SIZE), scaled_gram(orb_ref[...], MU))
    out_ref[...] = sweep_blocks(system, 0, FIRST_PART)


def inverse_third_kernel(part_ref, out_ref):
    out_ref[...] = -sweep_blocks(part_ref[...], FIRST_PART, RANK)


def packed_gram_kernel(rows_ref, gram_ref, copy_ref):
    gram_ref[...] = pack(gram_of(rows_ref[...]))
    copy_ref[...] = rows_ref[...]


def gram_kernel(rows_ref, gram_ref):
    gram_ref[...] = gram_of(rows_ref[...])


def solve_first_kernel(terms_ref, inverse_ref, out_ref, gram_ref):
    out_ref[...] = dot32(terms_ref[...], inverse_ref[...])
    gram_ref[...] = gram_of(out_ref[...])


def solve_second_kernel(terms_ref, inverse_ref, scale_ref, out_ref, slab_ref, gram_ref):
    out_ref[...] = dot32(terms_ref[...] / scale_ref[...], inverse_ref[...])
    gram_ref[...] = gram_of(out_ref[...])
    count = slab_ref.shape[1]
    slab = gram_ref[pl.ds(pl.multiple_of(lax.axis_index("aux") * count, count), count), :]
    slab_ref[...] = jnp.broadcast_to(slab[None], slab_ref.shape)


def solve_third_kernel(terms_ref, inverse_ref, scale_ref, out_ref):
    values = dot32(terms_ref[...] / scale_ref[...], inverse_ref[...])
    squares = jnp.sum(values * values, axis=0, keepdims=True)
    out_ref[...] = values / jnp.sqrt(squares * (1.0 / NU) + epsilon)


def whole(kernel, out_shape, *operands, flops=10**9, scratch=()):
    return pl.pallas_call(
        kernel,
        out_shape=out_shape,
        scratch_shapes=scratch,
        compiler_params=params,
        cost_estimate=pl.CostEstimate(flops=flops, bytes_accessed=10**6, transcendentals=0),
        name=kernel.__name__.removesuffix("_kernel"),
    )(*operands)


def in_hbm(operand):
    return pltpu.with_memory_space_constraint(operand, pltpu.HBM)


def exchange(pieces, axis):
    return lax.all_to_all(pieces, axis, 0, 0)


def spread(piece, axis):
    count = lax.axis_size(axis)
    return exchange(jnp.broadcast_to(piece[None], (count,) + piece.shape), axis)


def beside(pieces, slab):
    filling = jnp.broadcast_to(slab[None], pieces.shape[:1] + slab.shape)
    return lax.dynamic_update_slice(pieces, filling, (0, pieces.shape[1] - slab.shape[0], 0))


def per_device(tiles, tile_list, orb_factor, nu_factor):
    n_aux = lax.axis_size("aux")
    n_orb = lax.axis_size("orb")
    m_orb = 512 // n_orb
    m_aux = 512 // n_aux
    g_aux = RANK // n_aux
    g_orb = PACKED.shape[0] // n_orb

    tile_list = in_hbm(tile_list)
    gram_orb, orb_factor = whole(packed_gram_kernel, (PACKED, ROWS), in_hbm(orb_factor))
    slab_orb = jnp.sum(exchange(gram_orb.reshape(n_orb, g_orb, RANK), "orb"), axis=0)
    partial_first = over_tiles(
        first_body, tile_list, tiles, orb_factor, in_hbm(nu_factor), n_orb, g_orb
    )
    nu_later, slab_orb = lax.optimization_barrier((nu_factor, slab_orb))
    received = exchange(beside(partial_first, slab_orb), "orb")
    gram_nu = whole(gram_kernel, SQUARE, nu_later)
    gram_orb = received[:, m_orb:].reshape(PACKED.shape)
    first_terms = spread(jnp.sum(received[:, :m_orb], axis=0), "orb").reshape(512, RANK)
    inverse_first = whole(inverse_first_kernel, SQUARE, gram_orb, gram_nu, flops=10**10)

    a_new, gram_part = whole(solve_first_kernel, (ROWS, SQUARE), first_terms, inverse_first)
    slab_aux = jnp.sum(exchange(gram_part.reshape(n_aux, g_aux, RANK), "aux"), axis=0)
    partial_second = over_tiles(second_body, tile_list, tiles, a_new, nu_factor, n_aux, g_aux)
    received = exchange(beside(partial_second, slab_aux), "aux")
    gram_aux = received[:, m_aux:].reshape(RANK, RANK)
    second_terms = spread(jnp.sum(received[:, :m_aux], axis=0), "aux").reshape(512, RANK)
    inverse_second, scale_first = whole(
        inverse_second_kernel, (SQUARE, LINE), gram_aux, gram_nu, flops=10**10
    )

    b_new, slabs = whole(
        solve_second_kernel,
        (ROWS, jax.ShapeDtypeStruct((n_orb, g_aux, RANK), f32)),
        second_terms,
        inverse_second,
        scale_first,
        scratch=(pltpu.VMEM((RANK, RANK), f32),),
    )
    slab_orb = jnp.sum(exchange(slabs, "orb"), axis=0)
    partial_third = over_tiles(third_body, tile_list, tiles, a_new, b_new, n_aux, g_aux)
    received = exchange(beside(partial_third, slab_orb), "aux")
    gram_orb = received[:, m_aux:].reshape(RANK, RANK)
    begun, scale_second, scale_both = whole(
        begin_third_kernel, (SQUARE, LINE, LINE), gram_aux, gram_orb, flops=5 * 10**9
    )
    pieces = spread(jnp.sum(received[:, :m_aux], axis=0), "orb")
    pieces, begun = lax.optimization_barrier((pieces, begun))
    third_terms = spread(jnp.sum(pieces, axis=0), "aux").reshape(512, RANK)
    inverse_third = whole(inverse_third_kernel, SQUARE, begun, flops=5 * 10**9)
    nu_updated = whole(solve_third_kernel, ROWS, third_terms, inverse_third, scale_both)
    return (a_new / scale_first, b_new / scale_second, nu_updated)


def solution(mesh):
    return jax.shard_map(
        per_device,
        mesh=mesh,
        in_specs=(P(("aux", "orb"), None, None), P(None, ("aux", "orb")), P("orb", None), P()),
        out_specs=(P("aux", None), P("orb", None), P()),
        check_vma=False,
    )
```
